256 devices in a mesh: batch: 16 (over z_hi, y, core), dap: 16 (over z_lo, x).
Axes of the slice: x: 4, y: 4, z: 8 (z_hi: 2, z_lo: 4; z = z_hi * 4 + z_lo), core: 2. Of those that a mesh axis runs over, the one named last changes fastest.
Arguments:
- alignment: bfloat16 [32, 128, 256, 256], P('batch', 'dap'), may hold values from -6 to 6
- cotangent: bfloat16 [32, 128, 256, 256], P('batch', 'dap'), may hold values from -6 to 6
- query_weight: bfloat16 [256, 256], replicated, may hold values from -3 to 3
- key_weight: bfloat16 [256, 256], replicated, may hold values from -3 to 3
- value_weight: bfloat16 [256, 256], replicated, may hold values from -0.375 to 0.375
- gate_weight: bfloat16 [256, 256], replicated, may hold values from -0.375 to 0.375
- gate_bias: float32 [256], replicated, may hold values from -4 to 4
- out_weight: bfloat16 [256, 256], replicated, may hold values from -0.375 to 0.375
- out_bias: float32 [256], replicated, may hold values from -3 to 3
- ln_gain: float32 [256], replicated, may hold values from 0.1 to 1.9
- ln_bias: float32 [256], replicated, may hold values from -3 to 3
Outputs:
- updated: bfloat16 [32, 128, 256, 256], P('batch', 'dap')
- grad_alignment: bfloat16 [32, 128, 256, 256], P('batch', 'dap')
- grad_projections: float32 [4, 256, 256], replicated
- grad_output: float32 [256, 256], replicated
- grad_vectors: float32 [4, 256], replicated
The draws below stay inside these ranges and needn't reach their ends.
All inputs are finite; a program needn't handle non-finite values.
Results may differ from the reference program's by a relative error of at most 0.012.
The reference program's roundings to bfloat16 on the way (of `normed`, `soft_half`, `gated` and `d_scores`) count: a program that leaves them out, or rounds other values in their place, can miss the bound.
Values may be sent and summed in bfloat16 or wider, within the bound.
No kernel may reach another device: no remote copies, remote signals or barrier semaphores. Data moves between devices by JAX's collectives and lax.ppermute only.
A program may use at most 128 MiB of HBM per device.

```python
import math
import jax
import jax.numpy as jnp
from jax import lax

C = 256
HEADS = 8
HDIM = 32
ROWS = 128
RES = 256
HD = 256
STRUCTS = 32


def shared_base(key):
    return jax.random.normal(key, (C, HEADS * HDIM), jnp.float32)


def draw_query_weight(key, part):
    base = shared_base(key)
    key = jax.random.fold_in(key, 11)
    own = jax.random.normal(key, (C, HEADS * HDIM), jnp.float32)
    values = (0.5 * base + 0.866 * own) * C ** (-0.5)
    return jnp.clip(values, -3.0, 3.0).astype(jnp.bfloat16)


def draw_key_weight(key, part):
    base = shared_base(key)
    key = jax.random.fold_in(key, 12)
    own = jax.random.normal(key, (C, HEADS * HDIM), jnp.float32)
    values = (0.5 * base + 0.866 * own) * C ** (-0.5)
    return jnp.clip(values, -3.0, 3.0).astype(jnp.bfloat16)


def strengthened(values, rng, source, target, blocks, factor):
    def block_of(position):
        return (jnp.arange(values.shape[position]) // (values.shape[position] // blocks)).reshape((-1,) + (1,) * (values.ndim - 1 - position))

    one_side = jax.random.permutation(rng, blocks)[block_of(target)]
    far = (block_of(target) + blocks // 2) % blocks
    return jnp.where((block_of(source) == one_side) | (block_of(source) == far), factor * values, values)


def block_scale(stream_key, shape, shards, least, largest):
    def one(position, parts):
        draws = jax.random.uniform(jax.random.fold_in(jax.random.fold_in(stream_key, 6), position), (parts,), jnp.float32, least / len(shards), largest / len(shards))
        return jnp.repeat(jnp.exp(draws), shape[position] // parts).reshape((-1,) + (1,) * (len(shape) - position - 1))

    gain = one(*shards[0])
    for cut in shards[1:]:
        gain = gain * one(*cut)
    return gain


def gaussian(stream_key, dims, scale, limit, split=(), dtype=jnp.bfloat16):
    level = block_scale(stream_key, dims, split, -0.22, 0.18) if split else 1.0
    values = jax.random.normal(stream_key, dims, jnp.float32) * scale * level
    return jnp.minimum(jnp.maximum(values, -limit), limit).astype(dtype)


def gaussian_with(own_key, dims, spread, bound, shards, heavy, dtype=jnp.bfloat16):
    array = spread * jax.random.normal(own_key, dims, jnp.float32)
    if shards:
        array = array * block_scale(own_key, dims, shards, -0.22, 0.18)
    return jnp.clip(strengthened(array, jax.random.fold_in(own_key, 3), *heavy), -bound, bound).astype(dtype)


def setup_inputs(seed: int = 0) -> dict:
    streams_of = jax.random.split(jax.random.key(seed), 12)
    return {
        "alignment": gaussian(streams_of[0], (STRUCTS, ROWS, RES, C), 1.0, 6.0, ((0, 16), (1, 16))),
        "cotangent": gaussian_with(streams_of[1], (STRUCTS, ROWS, RES, C), 1.0, 6.0, ((0, 16), (1, 16)), (0, 3, 16, 2.0)),
        "query_weight": draw_query_weight(jax.random.fold_in(streams_of[11], 71), 0),
        "key_weight": draw_key_weight(jax.random.fold_in(streams_of[11], 71), 0),
        "value_weight": gaussian(streams_of[4], (C, HD), C ** -0.5, 0.375),
        "gate_weight": gaussian(streams_of[5], (C, HD), C ** -0.5, 0.375),
        "gate_bias": gaussian(streams_of[6], (HD,), 1.0, 4.0, (), jnp.float32),
        "out_weight": gaussian(streams_of[7], (HD, C), HD ** -0.5, 0.375),
        "out_bias": gaussian(streams_of[8], (C,), 0.5, 3.0, (), jnp.float32),
        "ln_gain": jnp.clip(1.0 + 0.18 * jax.random.normal(streams_of[9], (C,), jnp.float32), 0.1, 1.9),
        "ln_bias": gaussian(streams_of[10], (C,), 0.5, 3.0, (), jnp.float32),
    }


EPSILON = 1e-05

def contract(form, left, right):
    return jnp.einsum(form, left.astype(jnp.float32), right.astype(jnp.float32))

def column_block(columns, upstream, params):
    query_weight, key_weight, value_weight, gate_weight, gate_bias, out_weight, out_bias, ln_gain, ln_bias = params
    row_count, col_count = (columns.shape[0], columns.shape[1])
    inputs = columns.astype(jnp.float32)
    centered = inputs - lax.optimization_barrier(jnp.mean(inputs, axis=-1, keepdims=True))
    inv_std = lax.rsqrt(lax.optimization_barrier(jnp.mean(centered * centered, axis=-1, keepdims=True)) + EPSILON)
    standard = centered * inv_std
    normed = (standard * ln_gain + ln_bias).astype(jnp.bfloat16)
    in_weights = jnp.concatenate([query_weight, key_weight, value_weight, gate_weight], axis=1)
    projected = contract('irc,cf->irf', normed, in_weights)
    inv_scale = 1.0 / math.sqrt(HDIM)
    split_shape = (row_count, col_count, HEADS, HDIM)
    queries = (projected[..., :HD] * inv_scale).astype(jnp.bfloat16).reshape(split_shape)
    key_rows = projected[..., HD:2 * HD].astype(jnp.bfloat16).reshape(split_shape)
    value_rows = projected[..., 2 * HD:3 * HD].astype(jnp.bfloat16).reshape(split_shape)
    gate_open = jax.nn.sigmoid(projected[..., 3 * HD:] + gate_bias)
    scores = contract('irhd,jrhd->rhij', queries, key_rows)
    shifted = jnp.exp(scores - lax.optimization_barrier(jnp.max(scores, axis=-1, keepdims=True)))
    soft = shifted / lax.optimization_barrier(jnp.sum(shifted, axis=-1, keepdims=True))
    soft_half = soft.astype(jnp.bfloat16)
    attended = contract('rhij,jrhd->irhd', soft_half, value_rows).reshape(row_count, col_count, HD)
    gated = (gate_open * attended).astype(jnp.bfloat16)
    update = contract('irf,fc->irc', gated, out_weight) + out_bias
    updated = (inputs + update).astype(jnp.bfloat16)
    d_gated = contract('irc,fc->irf', upstream, out_weight)
    d_attended = (d_gated * gate_open).astype(jnp.bfloat16).reshape(split_shape)
    d_logit = (d_gated * attended * gate_open * (1.0 - gate_open)).astype(jnp.bfloat16)
    d_soft = contract('irhd,jrhd->rhij', d_attended, value_rows)
    d_scores = (soft * (d_soft - lax.optimization_barrier(jnp.sum(soft * d_soft, axis=-1, keepdims=True)))).astype(jnp.bfloat16)
    d_queries = (contract('rhij,jrhd->irhd', d_scores, key_rows) * inv_scale).astype(jnp.bfloat16)
    d_keys = contract('rhij,irhd->jrhd', d_scores, queries).astype(jnp.bfloat16)
    d_values = contract('rhij,irhd->jrhd', soft_half, d_attended).astype(jnp.bfloat16)
    flat_shape = (row_count, col_count, HD)
    d_projected = jnp.concatenate([d_queries.reshape(flat_shape), d_keys.reshape(flat_shape), d_values.reshape(flat_shape), d_logit], axis=-1)
    d_normed = contract('irf,cf->irc', d_projected, in_weights)
    grad_in = contract('irc,irf->cf', normed, d_projected).reshape(C, 4, HD).transpose(1, 0, 2)
    grad_out = contract('irf,irc->fc', gated, upstream)
    d_hat = d_normed * ln_gain
    branch = inv_std * (d_hat - lax.optimization_barrier(jnp.mean(d_hat, axis=-1, keepdims=True)) - standard * lax.optimization_barrier(jnp.mean(d_hat * standard, axis=-1, keepdims=True)))
    grad_cols = (upstream.astype(jnp.float32) + branch).astype(jnp.bfloat16)
    vectors = jnp.stack([lax.optimization_barrier(jnp.sum(d_logit.astype(jnp.float32), axis=(0, 1))), lax.optimization_barrier(jnp.sum(upstream.astype(jnp.float32), axis=(0, 1))), lax.optimization_barrier(jnp.sum(d_normed * standard, axis=(0, 1))), lax.optimization_barrier(jnp.sum(d_normed, axis=(0, 1)))])
    return (updated, grad_cols, grad_in, grad_out, vectors)

def reference(alignment, cotangent, query_weight, key_weight, value_weight, gate_weight, gate_bias, out_weight, out_bias, ln_gain, ln_bias):
    params = (query_weight, key_weight, value_weight, gate_weight, gate_bias, out_weight, out_bias, ln_gain, ln_bias)

    def one_structure(carry, pair):
        updated, grad_cols, grad_in, grad_out, vectors = column_block(pair[0], pair[1], params)
        return ((carry[0] + grad_in, carry[1] + grad_out, carry[2] + vectors), (updated, grad_cols))
    start = (jnp.zeros((4, C, HD), jnp.float32), jnp.zeros((HD, C), jnp.float32), jnp.zeros((4, C), jnp.float32))
    sums, outputs = lax.scan(one_structure, start, (alignment, cotangent))
    factor = 1.0 / math.sqrt(STRUCTS * ROWS * RES)
    return (outputs[0], outputs[1], sums[0] * factor, sums[1] * factor, sums[2] * factor)
```

```python
import functools
import math

import jax
import jax.numpy as jnp
from jax import lax
from jax.experimental import pallas as pl
from jax.experimental.pallas import tpu as pltpu
from jax.sharding import Mesh
from jax.sharding import PartitionSpec as P

C = 256
HEADS = 8
HDIM = 32
ROWS = 128
RES = 256
HD = 256
STRUCTS = 32
EPSILON = 1e-05
INV_SCALE = 1.0 / math.sqrt(HDIM)
FACTOR = 1.0 / math.sqrt(STRUCTS * ROWS * RES)
F32 = jnp.float32
BF16 = jnp.bfloat16

MEMBERS = 16
OWN_ROWS = ROWS // MEMBERS
OWN_RES = RES // MEMBERS
PAIRS = OWN_RES // 2
DAP = ("z_lo", "x")
BATCH = ("z_hi", "y", "core")
RING = ("z_hi", "z_lo")
TILES = 352
GROUP = 4


def dot(left, right, left_dim=1, right_dim=0):
    return lax.dot_general(
        left, right, (((left_dim,), (right_dim,)), ((), ())), preferred_element_type=F32
    )


def pack_kernel(x_ref, cot_ref, out_ref, wide):
    count = GROUP * OWN_RES
    for which, ref in enumerate((x_ref, cot_ref)):
        for row in range(OWN_ROWS):
            for side in range(2):
                wide[side, pl.ds(row, count, stride=OWN_ROWS), :] = ref[
                    0, row, :, side * 128 : side * 128 + 128
                ].astype(F32)
        for side in range(2):
            out_ref[:, which, :, :, side * 128 : side * 128 + 128] = (
                wide[side].reshape(GROUP, PAIRS, 16, 128).astype(BF16)
            )


def pack(alignment, cotangent, struct):
    block = pl.BlockSpec((1, OWN_ROWS, GROUP * OWN_RES, C), lambda g: (struct, 0, g, 0))
    return pl.pallas_call(
        pack_kernel,
        grid=(MEMBERS // GROUP,),
        in_specs=[block, block],
        out_specs=pl.BlockSpec((GROUP, 2, PAIRS, 16, C), lambda g: (g, 0, 0, 0, 0)),
        out_shape=jax.ShapeDtypeStruct((MEMBERS, 2, PAIRS, 16, C), BF16),
        scratch_shapes=[pltpu.VMEM((2, GROUP * OWN_RES * OWN_ROWS, 128), F32)],
        compiler_params=pltpu.CompilerParams(vmem_limit_bytes=16 * 2**20),
        cost_estimate=pl.CostEstimate(flops=0, bytes_accessed=2**22, transcendentals=0),
    )(alignment, cotangent)


def unpack_kernel(*refs):
    in_ref, upd_ref, grad_ref, wide = refs[0], *refs[-3:]
    count = GROUP * OWN_RES
    for which, ref in enumerate((upd_ref, grad_ref)):
        for side in range(2):
            lanes = slice(side * 128, side * 128 + 128)
            wide[side] = in_ref[:, which, :, :, lanes].astype(F32).reshape(count * OWN_ROWS, 128)
            for row in range(OWN_ROWS):
                ref[0, row, :, lanes] = wide[
                    side, pl.ds(row, count, stride=OWN_ROWS), :
                ].astype(BF16)


def unpack(packed, struct, structs, earlier):
    block = pl.BlockSpec((1, OWN_ROWS, GROUP * OWN_RES, C), lambda g: (struct, 0, g, 0))
    shape = jax.ShapeDtypeStruct((structs, OWN_ROWS, RES, C), BF16)
    return pl.pallas_call(
        unpack_kernel,
        grid=(MEMBERS // GROUP,),
        in_specs=[pl.BlockSpec((GROUP, 2, PAIRS, 16, C), lambda g: (g, 0, 0, 0, 0))]
        + [pl.BlockSpec(memory_space=pl.ANY)] * len(earlier),
        out_specs=[block, block],
        out_shape=[shape, shape],
        input_output_aliases={1 + k: k for k in range(len(earlier))},
        scratch_shapes=[pltpu.VMEM((2, GROUP * OWN_RES * OWN_ROWS, 128), F32)],
        compiler_params=pltpu.CompilerParams(vmem_limit_bytes=16 * 2**20),
        cost_estimate=pl.CostEstimate(flops=0, bytes_accessed=2**22, transcendentals=0),
    )(packed, *earlier)


def token_rows(block):
    wide = block.astype(F32)
    return jnp.concatenate([wide[:, :8].reshape(ROWS, C), wide[:, 8:].reshape(ROWS, C)], axis=0)


def row_blocks(tokens):
    return jnp.concatenate(
        [tokens[:ROWS].reshape(MEMBERS, 8, C), tokens[ROWS:].reshape(MEMBERS, 8, C)], axis=1
    )


def fold_rows(tokens):
    return jnp.sum(tokens.reshape(tokens.shape[0] // 8, 8, C), axis=0)


def tiles_of(matrix):
    count = matrix.shape[0] // 8
    return matrix[:, :128].reshape(count, 8, 128), matrix[:, 128:].reshape(count, 8, 128)


def pair_kernel(steps, has_earlier, *refs):
    x_ref, cot_ref, w_ref, wt_ref, wo_ref, gb_ref, rows_ref = refs[:7]
    out_ref, sums_ref, qc, kc, vc, dac, attc, dprojc, gin, gout, vec, dlog = refs[-12:]

    @pl.when(pl.program_id(0) == 0)
    def _():
        gin[...] = jnp.zeros_like(gin)
        gout[...] = jnp.zeros_like(gout)
        vec[...] = jnp.zeros_like(vec)
        dlog[...] = jnp.zeros_like(dlog)

    out_bias, gain, bias = rows_ref[0:1], rows_ref[1:2], rows_ref[2:3]
    x = token_rows(x_ref[:, 0, 0])
    cot = token_rows(cot_ref[:, 0, 0])
    cot_half = cot.astype(BF16)
    centered = x - jnp.mean(x, axis=-1, keepdims=True)
    inv_std = lax.rsqrt(jnp.mean(centered * centered, axis=-1, keepdims=True) + EPSILON)
    standard = centered * inv_std
    normed = (standard * gain + bias).astype(BF16)

    kv = dot(normed, w_ref[:, HD : 3 * HD]).astype(BF16)
    proj = dot(wt_ref[...], normed, 1, 1)
    qc[...] = (proj[:HD] * INV_SCALE).astype(BF16)
    kc[...] = proj[HD : 2 * HD].astype(BF16)
    vc[...] = proj[2 * HD : 3 * HD].astype(BF16)
    gate = jax.nn.sigmoid(proj[3 * HD :] + jnp.concatenate([gb_ref[...]] * 2, axis=1))
    d_gated = dot(wo_ref[...], cot_half, 1, 1)
    dac[...] = (d_gated * gate).astype(BF16)

    head_of_lane = lax.broadcasted_iota(jnp.int32, (1, 128), 1) // HDIM
    for r in range(2):
        toks = slice(r * ROWS, (r + 1) * ROWS)
        for half in range(2):
            lanes = slice(half * 128, half * 128 + 128)
            k_half = kv[toks, half * 128 : half * 128 + 128]
            v_half = kv[toks, HD + half * 128 : HD + half * 128 + 128]
            zero = jnp.zeros_like(k_half)
            k_stack = jnp.concatenate(
                [jnp.where(head_of_lane == h, k_half, zero) for h in range(4)], axis=0
            )
            v_stack = jnp.concatenate(
                [jnp.where(head_of_lane == h, v_half, zero) for h in range(4)], axis=0
            )
            scores = dot(k_stack, qc[lanes, toks])
            d_softs = dot(v_stack, dac[lanes, toks])
            for h in range(4):
                s = scores[h * 128 : h * 128 + 128]
                shifted = jnp.exp(s - jnp.max(s, axis=0, keepdims=True))
                soft = shifted * (1.0 / jnp.sum(shifted, axis=0, keepdims=True))
                soft_half = soft.astype(BF16)
                weighted = soft * d_softs[h * 128 : h * 128 + 128]
                d_s = (weighted - soft * jnp.sum(weighted, axis=0, keepdims=True)).astype(BF16)
                f = half * 128 + h * HDIM
                chans = slice(f, f + HDIM)
                attc[chans, toks] = dot(vc[chans, toks], soft_half)
                dprojc[chans, toks] = (dot(kc[chans, toks], d_s) * INV_SCALE).astype(BF16)
                dprojc[HD + f : HD + f + HDIM, toks] = dot(qc[chans, toks], d_s, 1, 1).astype(BF16)
                dprojc[2 * HD + f : 2 * HD + f + HDIM, toks] = dot(
                    dac[chans, toks], soft_half, 1, 1
                ).astype(BF16)

    gated = gate * attc[...]
    d_logit = (d_gated * gated * (1.0 - gate)).astype(BF16)
    dprojc[3 * HD :, :] = d_logit
    gated_half = gated.astype(BF16)
    dlog[...] += d_logit.astype(F32)[:, :128] + d_logit.astype(F32)[:, 128:]
    gin[...] += dot(dprojc[...], normed)
    gout[...] += dot(gated_half, cot_half)
    update = dot(gated_half.T, wo_ref[...]) + out_bias
    out_ref[:, 0, 0] = row_blocks(x + update).astype(BF16)
    d_normed = dot(w_ref[...], dprojc[...]).T
    d_hat = d_normed * gain
    d_std = d_normed * standard
    branch = inv_std * (
        d_hat
        - jnp.mean(d_hat, axis=-1, keepdims=True)
        - standard * jnp.mean(d_hat * standard, axis=-1, keepdims=True)
    )
    out_ref[:, 1, 0] = row_blocks(cot + branch).astype(BF16)
    vec[0] += fold_rows(cot)
    vec[1] += fold_rows(d_std)
    vec[2] += fold_rows(d_normed)

    @pl.when(pl.program_id(0) == steps - 1)
    def _():
        def put(first, tiles):
            count = tiles.shape[0]
            if has_earlier:
                tiles = tiles + refs[7][first : first + count]
            sums_ref[first : first + count] = tiles

        for block in range(5):
            matrix = gin[block * HD : (block + 1) * HD].T if block < 4 else gout[...]
            left, right = tiles_of(matrix)
            put(block * 32, left)
            put(160 + block * 32, right)
        rows = [jnp.sum(dlog[...].T, axis=0, keepdims=True)] + [
            jnp.sum(vec[k], axis=0, keepdims=True) for k in range(3)
        ]
        vectors = [row[:, side : side + 128] for row in rows for side in (0, 128)]
        put(320, jnp.concatenate(vectors, axis=0)[None])
        sums_ref[321:] = jnp.zeros((TILES - 321, 8, 128), F32)


def columns(packed, params, earlier):
    def part(which):
        return pl.BlockSpec((MEMBERS, 1, 1, 16, C), lambda p: (0, which, p, 0, 0))

    def whole(shape):
        return pl.BlockSpec(shape, lambda p: (0,) * len(shape))

    pairs = packed.shape[2]
    wide = (HD, 2 * ROWS)
    return pl.pallas_call(
        functools.partial(pair_kernel, pairs, bool(earlier)),
        grid=(pairs,),
        in_specs=[part(0), part(1)] + [whole(a.shape) for a in (*params, *earlier)],
        out_specs=[
            pl.BlockSpec((MEMBERS, 2, 1, 16, C), lambda p: (0, 0, p, 0, 0)),
            whole((TILES, 8, 128)),
        ],
        out_shape=[
            jax.ShapeDtypeStruct(packed.shape, BF16),
            jax.ShapeDtypeStruct((TILES, 8, 128), F32),
        ],
        scratch_shapes=[pltpu.VMEM(wide, BF16)] * 4
        + [
            pltpu.VMEM(wide, F32),
            pltpu.VMEM((4 * HD, 2 * ROWS), BF16),
            pltpu.VMEM((4 * HD, C), F32),
            pltpu.VMEM((HD, C), F32),
            pltpu.VMEM((3, 8, C), F32),
            pltpu.VMEM((HD, 128), F32),
        ],
        compiler_params=pltpu.CompilerParams(
            dimension_semantics=("arbitrary",), vmem_limit_bytes=32 * 2**20
        ),
        cost_estimate=pl.CostEstimate(
            flops=pairs * 4_000_000_000, bytes_accessed=2**23, transcendentals=pairs * 300_000
        ),
    )(packed, packed, *params, *earlier)


def shift(value, axes, size, step):
    return lax.ppermute(value, axes, [(k, (k + step) % size) for k in range(size)])


def scatter_sum(value, axes, size):
    own = lax.axis_index(axes)
    count = value.shape[0] // size

    def block_for(step):
        return lax.dynamic_slice_in_dim(value, lax.rem(own + step, size) * count, count, 0)

    arrived = [shift(block_for(step), axes, size, step) for step in range(1, size)]
    return functools.reduce(jnp.add, arrived, block_for(0))


def gather(value, axes, size):
    own = lax.axis_index(axes)
    count = value.shape[0]
    arrived = [shift(value, axes, size, step) for step in range(1, size)]
    turned = jnp.concatenate(([*reversed(arrived), value]) * 2, axis=0)
    return lax.dynamic_slice_in_dim(turned, (size - 1 - own) * count, size * count, 0)


def all_sum(tiles):
    stages = (("core", 2), ("y", 4), ("x", 4))
    for axes, size in stages:
        tiles = scatter_sum(tiles, axes, size)
    count = tiles.shape[0]
    tiles = jnp.concatenate([tiles, jnp.zeros((16 - count, 8, 128), F32)], axis=0)
    tiles = gather(scatter_sum(tiles, RING, 8) * FACTOR, RING, 8)[:count]
    for axes, size in reversed(stages):
        tiles = gather(tiles, axes, size)
    return tiles


def shards(alignment, cotangent, wq, wk, wv, wg, gate_bias, wo, out_bias, gain, bias):
    structs = alignment.shape[0]
    w = jnp.concatenate([wq, wk, wv, wg], axis=1)
    rows = jnp.concatenate([jnp.stack([out_bias, gain, bias]), jnp.zeros((5, C), F32)], axis=0)
    params = (w, w.T, wo, jnp.broadcast_to(gate_bias[:, None], (HD, 128)), rows)

    def exchange(value):
        return lax.all_to_all(value, DAP, 0, 0, tiled=True)

    arrived = [exchange(pack(alignment, cotangent, s)) for s in range(structs)]
    sums, done = (), ()
    leaving = []
    for s in range(structs):
        results, tiles = columns(arrived[s], params, sums)
        sums = (tiles,)
        leaving.append(exchange(results))
    for s in range(structs):
        done = tuple(unpack(leaving[s], s, structs, done))
    totals = all_sum(sums[0])
    matrices = jnp.concatenate(
        [totals[:160].reshape(5 * HD, 128), totals[160:320].reshape(5 * HD, 128)], axis=1
    ).reshape(5, HD, C)
    vectors = totals[320].reshape(4, C)
    return (*done, matrices[:4], matrices[4], vectors)


def solution(mesh):
    parts = Mesh(mesh.devices.reshape(2, 4, 2, 4, 4), BATCH + DAP)
    split = P(BATCH, DAP, None, None)
    return jax.shard_map(
        shards,
        mesh=parts,
        in_specs=(split, split) + (P(),) * 9,
        out_specs=(split, split, P(), P(), P()),
        check_vma=False,
    )
```

```python
import functools
import math

import jax
import jax.numpy as jnp
from jax import lax
from jax.experimental import pallas as pl
from jax.experimental.pallas import tpu as pltpu
from jax.sharding import Mesh
from jax.sharding import PartitionSpec as P

C = 256
HEADS = 8
HDIM = 32
ROWS = 128
RES = 256
HD = 256
STRUCTS = 32
EPSILON = 1e-05
INV_SCALE = 1.0 / math.sqrt(HDIM)
FACTOR = 1.0 / math.sqrt(STRUCTS * ROWS * RES)
F32 = jnp.float32
BF16 = jnp.bfloat16

MEMBERS = 16
OWN_ROWS = ROWS // MEMBERS
QUADS = 2
PAIRS = 4
HALF_RES = RES // QUADS
DAP = ("z_lo", "x")
BATCH = ("z_hi", "y", "core")
TILES = 352
GROUP = 8
COUNT = GROUP * 2 * PAIRS
VMEM = 60 * 2**20


def dot(left, right, left_dim=1, right_dim=0):
    return lax.dot_general(
        left, right, (((left_dim,), (right_dim,)), ((), ())), preferred_element_type=F32
    )


def quad_specs(first):
    rows = pl.BlockSpec(
        (1, OWN_ROWS, COUNT, C),
        lambda n, g: ((first + n) // QUADS, 0, (first + n) % QUADS * (MEMBERS // GROUP) + g, 0),
    )
    packed = pl.BlockSpec((GROUP, 2, PAIRS, 16, C), lambda n, g: (g, 0, n, 0, 0))
    return rows, packed


def pack_kernel(x_ref, cot_ref, out_ref, wide):
    for which, ref in enumerate((x_ref, cot_ref)):
        for side in range(2):
            lanes = slice(side * 128, side * 128 + 128)
            for row in range(OWN_ROWS):
                wide[which, side, pl.ds(row, COUNT, stride=OWN_ROWS), :] = ref[0, row, :, lanes].astype(F32)
            out_ref[:, which, :, :, lanes] = wide[which, side].reshape(GROUP, PAIRS, 16, 128).astype(BF16)


def pack(alignment, cotangent, first, quads):
    rows, packed = quad_specs(first)
    return pl.pallas_call(
        pack_kernel,
        grid=(quads, MEMBERS // GROUP),
        in_specs=[rows, rows],
        out_specs=packed,
        out_shape=pltpu.HBM((MEMBERS, 2, quads * PAIRS, 16, C), BF16),
        scratch_shapes=[pltpu.VMEM((2, 2, COUNT * OWN_ROWS, 128), F32)],
        compiler_params=pltpu.CompilerParams(vmem_limit_bytes=VMEM),
        cost_estimate=pl.CostEstimate(flops=0, bytes_accessed=quads * 2**21, transcendentals=0),
    )(alignment, cotangent)


def unpack_kernel(*refs):
    in_ref, upd_ref, grad_ref, wide = refs[0], *refs[-3:]
    for which, ref in enumerate((upd_ref, grad_ref)):
        for side in range(2):
            lanes = slice(side * 128, side * 128 + 128)
            wide[which, side] = in_ref[:, which, :, :, lanes].astype(F32).reshape(COUNT * OWN_ROWS, 128)
            for row in range(OWN_ROWS):
                ref[0, row, :, lanes] = wide[
                    which, side, pl.ds(row, COUNT, stride=OWN_ROWS), :
                ].astype(BF16)


def unpack(packed, first, structs, earlier):
    rows, blocks = quad_specs(first)
    shape = pltpu.HBM((structs, OWN_ROWS, RES, C), BF16)
    quads = packed.shape[2] // PAIRS
    return pl.pallas_call(
        unpack_kernel,
        grid=(quads, MEMBERS // GROUP),
        in_specs=[blocks] + [pl.BlockSpec(memory_space=pl.ANY)] * len(earlier),
        out_specs=[rows, rows],
        out_shape=[shape, shape],
        input_output_aliases={1 + k: k for k in range(len(earlier))},
        scratch_shapes=[pltpu.VMEM((2, 2, COUNT * OWN_ROWS, 128), F32)],
        compiler_params=pltpu.CompilerParams(vmem_limit_bytes=24 * 2**20),
        cost_estimate=pl.CostEstimate(flops=0, bytes_accessed=quads * 2**21, transcendentals=0),
    )(packed, *earlier)


def token_rows(block):
    wide = block.astype(F32)
    return jnp.concatenate([wide[:, :8].reshape(ROWS, C), wide[:, 8:].reshape(ROWS, C)], axis=0)


def row_blocks(tokens):
    return jnp.concatenate(
        [tokens[:ROWS].reshape(MEMBERS, 8, C), tokens[ROWS:].reshape(MEMBERS, 8, C)], axis=1
    )


def fold_rows(tokens):
    return jnp.sum(tokens.reshape(tokens.shape[0] // 8, 8, C), axis=0)


def tiles_of(matrix):
    count = matrix.shape[0] // 8
    return matrix[:, :128].reshape(count, 8, 128), matrix[:, 128:].reshape(count, 8, 128)


def pair_kernel(steps, early, has_earlier, *refs):
    x_ref, cot_ref, w_ref, wt_ref, wo_ref, gb_ref, rows_ref = refs[:7]
    early_ref = refs[-13]
    late_ref, sums_ref, qc, kc, vc, dac, attc, dprojc, gin, gout, vec, dlog = refs[-12:]

    @pl.when(pl.program_id(0) == 0)
    def _():
        gin[...] = jnp.zeros_like(gin)
        gout[...] = jnp.zeros_like(gout)
        vec[...] = jnp.zeros_like(vec)
        dlog[...] = jnp.zeros_like(dlog)

    out_bias, gain, bias = rows_ref[0:1], rows_ref[1:2], rows_ref[2:3]
    x = token_rows(x_ref[:, 0, 0])
    cot = token_rows(cot_ref[:, 0, 0])
    cot_half = cot.astype(BF16)
    centered = x - jnp.mean(x, axis=-1, keepdims=True)
    inv_std = lax.rsqrt(jnp.mean(centered * centered, axis=-1, keepdims=True) + EPSILON)
    standard = centered * inv_std
    normed = (standard * gain + bias).astype(BF16)

    kv = dot(normed, w_ref[:, HD : 3 * HD]).astype(BF16)
    proj = dot(wt_ref[...], normed, 1, 1)
    qc[...] = (proj[:HD] * INV_SCALE).astype(BF16)
    kc[...] = proj[HD : 2 * HD].astype(BF16)
    vc[...] = proj[2 * HD : 3 * HD].astype(BF16)
    gate = jax.nn.sigmoid(proj[3 * HD :] + jnp.concatenate([gb_ref[...]] * 2, axis=1))
    d_gated = dot(wo_ref[...], cot_half, 1, 1)
    dac[...] = (d_gated * gate).astype(BF16)

    head_of_lane = lax.broadcasted_iota(jnp.int32, (1, 128), 1) // HDIM
    for r in range(2):
        toks = slice(r * ROWS, (r + 1) * ROWS)
        for half in range(2):
            lanes = slice(half * 128, half * 128 + 128)
            k_half = kv[toks, half * 128 : half * 128 + 128]
            v_half = kv[toks, HD + half * 128 : HD + half * 128 + 128]
            zero = jnp.zeros_like(k_half)
            k_stack = jnp.concatenate(
                [jnp.where(head_of_lane == h, k_half, zero) for h in range(4)], axis=0
            )
            v_stack = jnp.concatenate(
                [jnp.where(head_of_lane == h, v_half, zero) for h in range(4)], axis=0
            )
            scores = dot(k_stack, qc[lanes, toks])
            d_softs = dot(v_stack, dac[lanes, toks])
            for h in range(4):
                s = scores[h * 128 : h * 128 + 128]
                shifted = jnp.exp(s - jnp.max(s, axis=0, keepdims=True))
                soft = shifted * (1.0 / jnp.sum(shifted, axis=0, keepdims=True))
                soft_half = soft.astype(BF16)
                weighted = soft * d_softs[h * 128 : h * 128 + 128]
                d_s = (weighted - soft * jnp.sum(weighted, axis=0, keepdims=True)).astype(BF16)
                f = half * 128 + h * HDIM
                chans = slice(f, f + HDIM)
                attc[chans, toks] = dot(vc[chans, toks], soft_half)
                dprojc[chans, toks] = (dot(kc[chans, toks], d_s) * INV_SCALE).astype(BF16)
                dprojc[HD + f : HD + f + HDIM, toks] = dot(qc[chans, toks], d_s, 1, 1).astype(BF16)
                dprojc[2 * HD + f : 2 * HD + f + HDIM, toks] = dot(
                    dac[chans, toks], soft_half, 1, 1
                ).astype(BF16)

    gated = gate * attc[...]
    d_logit = (d_gated * gated * (1.0 - gate)).astype(BF16)
    dprojc[3 * HD :, :] = d_logit
    gated_half = gated.astype(BF16)
    dlog[...] += d_logit.astype(F32)[:, :128] + d_logit.astype(F32)[:, 128:]
    gin[...] += dot(dprojc[...], normed)
    gout[...] += dot(gated_half, cot_half)
    update = dot(gated_half.T, wo_ref[...]) + out_bias
    updated = row_blocks(x + update).astype(BF16)
    d_normed = dot(w_ref[...], dprojc[...]).T
    d_hat = d_normed * gain
    d_std = d_normed * standard
    branch = inv_std * (
        d_hat
        - jnp.mean(d_hat, axis=-1, keepdims=True)
        - standard * jnp.mean(d_hat * standard, axis=-1, keepdims=True)
    )
    grad = row_blocks(cot + branch).astype(BF16)

    def store(ref):
        ref[:, 0, 0] = updated
        ref[:, 1, 0] = grad

    if early:
        pl.when(pl.program_id(0) < early)(lambda: store(early_ref))
        pl.when(pl.program_id(0) >= early)(lambda: store(late_ref))
    else:
        store(late_ref)
    vec[0] += fold_rows(cot)
    vec[1] += fold_rows(d_std)
    vec[2] += fold_rows(d_normed)

    @pl.when(pl.program_id(0) == steps - 1)
    def _():
        def put(first, tiles):
            count = tiles.shape[0]
            if has_earlier:
                tiles = tiles + refs[7][first : first + count]
            sums_ref[first : first + count] = tiles

        for block in range(5):
            matrix = gin[block * HD : (block + 1) * HD].T if block < 4 else gout[...]
            left, right = tiles_of(matrix)
            put(block * 32, left)
            put(160 + block * 32, right)
        rows = [jnp.sum(dlog[...].T, axis=0, keepdims=True)] + [
            jnp.sum(vec[k], axis=0, keepdims=True) for k in range(3)
        ]
        vectors = [row[:, side : side + 128] for row in rows for side in (0, 128)]
        put(320, jnp.concatenate(vectors, axis=0)[None])
        sums_ref[321:] = jnp.zeros((TILES - 321, 8, 128), F32)


def columns(packed, params, early, late, sums=None, filled=None):
    def part(which):
        return pl.BlockSpec((MEMBERS, 1, 1, 16, C), lambda p: (0, which, p, 0, 0))

    def whole(shape):
        return pl.BlockSpec(shape, lambda p: (0,) * len(shape))

    pairs = packed.shape[2]
    later = (sums, filled) if filled is not None else ()
    offset = late - pairs if later else -early
    out_block = (MEMBERS, 2, 1, 16, C)
    out_specs = [
        pl.BlockSpec(out_block, lambda p: (0, 0, jnp.maximum(p + offset, 0), 0, 0)),
        whole((TILES, 8, 128)),
    ]
    out_shape = [
        pltpu.HBM((MEMBERS, 2, late, 16, C), BF16),
        jax.ShapeDtypeStruct((TILES, 8, 128), F32),
    ]
    if early:
        out_specs.insert(0, pl.BlockSpec(out_block, lambda p: (0, 0, jnp.minimum(p, early - 1), 0, 0)))
        out_shape.insert(0, pltpu.HBM((MEMBERS, 2, early, 16, C), BF16))
    in_specs = [part(0), part(1)] + [whole(a.shape) for a in params]
    if later:
        in_specs += [whole(sums.shape), pl.BlockSpec(memory_space=pl.ANY)]
    wide = (HD, 2 * ROWS)
    return pl.pallas_call(
        functools.partial(pair_kernel, pairs, early, bool(later)),
        grid=(pairs,),
        in_specs=in_specs,
        out_specs=out_specs,
        out_shape=out_shape,
        input_output_aliases={len(in_specs) - 1: 0} if later else {},
        scratch_shapes=[pltpu.VMEM(wide, BF16)] * 4
        + [
            pltpu.VMEM(wide, F32),
            pltpu.VMEM((4 * HD, 2 * ROWS), BF16),
            pltpu.VMEM((4 * HD, C), F32),
            pltpu.VMEM((HD, C), F32),
            pltpu.VMEM((3, 8, C), F32),
            pltpu.VMEM((HD, 128), F32),
        ],
        compiler_params=pltpu.CompilerParams(
            dimension_semantics=("arbitrary",), vmem_limit_bytes=32 * 2**20
        ),
        cost_estimate=pl.CostEstimate(
            flops=pairs * 4_000_000_000, bytes_accessed=2**23, transcendentals=pairs * 300_000
        ),
    )(packed, packed, *params, *later)


def shift(value, axes, size, step):
    return lax.ppermute(value, axes, [(k, (k + step) % size) for k in range(size)])


def scatter_sum(value, axes, size):
    own = lax.axis_index(axes)
    count = value.shape[0] // size

    def block_for(step):
        return lax.dynamic_slice_in_dim(value, lax.rem(own + step, size) * count, count, 0)

    arrived = [shift(block_for(step), axes, size, step) for step in range(1, size)]
    return functools.reduce(jnp.add, arrived, block_for(0))


def gather(value, axes, size):
    own = lax.axis_index(axes)
    count = value.shape[0]
    arrived = [shift(value, axes, size, step) for step in range(1, size)]
    total = jnp.zeros((size * count, *value.shape[1:]), value.dtype)
    for step, piece in enumerate([value, *arrived]):
        place = lax.rem(own + size - step, size) * count
        total = lax.dynamic_update_slice_in_dim(total, piece, place, 0)
    return total


def swap_sum(value, axis, size, bit):
    return value + lax.ppermute(value, axis, [(k, k ^ bit) for k in range(size)])


def all_sum(tiles):
    stages = (("core", 2), ("y", 4), ("x", 4))
    for axes, size in stages:
        tiles = scatter_sum(tiles, axes, size)
    tiles = swap_sum(tiles, "z_lo", 4, 1)
    tiles = swap_sum(tiles, "z_lo", 4, 2)
    tiles = swap_sum(tiles, "z_hi", 2, 1) * FACTOR
    for axes, size in reversed(stages):
        tiles = gather(tiles, axes, size)
    return tiles


def shards(alignment, cotangent, wq, wk, wv, wg, gate_bias, wo, out_bias, gain, bias):
    structs = alignment.shape[0]
    w = jnp.concatenate([wq, wk, wv, wg], axis=1)
    rows = jnp.concatenate([jnp.stack([out_bias, gain, bias]), jnp.zeros((5, C), F32)], axis=0)
    params = (w, w.T, wo, jnp.broadcast_to(gate_bias[:, None], (HD, 128)), rows)

    def exchange(value):
        return lax.all_to_all(value, DAP, 0, 0, tiled=True)

    first = exchange(pack(alignment, cotangent, 0, 2))
    second = exchange(pack(alignment, cotangent, 2, 2))
    early, late, sums = columns(first, params, PAIRS, 3 * PAIRS)
    early = exchange(early)
    late, sums = columns(second, params, 0, 3 * PAIRS, sums, late)
    late = exchange(late)
    done = unpack(early, 0, structs, ())
    done = unpack(late, 1, structs, tuple(done))
    totals = all_sum(sums)
    matrices = jnp.concatenate(
        [totals[:160].reshape(5 * HD, 128), totals[160:320].reshape(5 * HD, 128)], axis=1
    ).reshape(5, HD, C)
    vectors = totals[320].reshape(4, C)
    return (*done, matrices[:4], matrices[4], vectors)


def solution(mesh):
    parts = Mesh(mesh.devices.reshape(2, 4, 2, 4, 4), BATCH + DAP)
    split = P(BATCH, DAP, None, None)
    return jax.shard_map(
        shards,
        mesh=parts,
        in_specs=(split, split) + (P(),) * 9,
        out_specs=(split, split, P(), P(), P()),
        check_vma=False,
    )
```

```python
import functools
import math

import jax
import jax.numpy as jnp
from jax import lax
from jax.experimental import pallas as pl
from jax.experimental.pallas import tpu as pltpu
from jax.sharding import Mesh
from jax.sharding import PartitionSpec as P

C = 256
HEADS = 8
HDIM = 32
ROWS = 128
RES = 256
HD = 256
STRUCTS = 32
EPSILON = 1e-05
INV_SCALE = 1.0 / math.sqrt(HDIM)
FACTOR = 1.0 / math.sqrt(STRUCTS * ROWS * RES)
F32 = jnp.float32
BF16 = jnp.bfloat16

MEMBERS = 16
OWN_ROWS = ROWS // MEMBERS
SIDE = 2 * MEMBERS
PAIRS = RES // SIDE
STEPS = 2
DAP = ("z_lo", "x")
BATCH = ("z_hi", "y", "core")
RING = ("z_hi", "z_lo")
TILES = 176
VMEM = 60 * 2**20


def dot(left, right, left_dim=1, right_dim=0):
    return lax.dot_general(
        left, right, (((left_dim,), (right_dim,)), ((), ())), preferred_element_type=F32
    )


def pair_specs(first, count):
    rows = pl.BlockSpec(
        (1, OWN_ROWS, count * SIDE, C),
        lambda n: ((first + n * count) // PAIRS, 0, (first + n * count) % PAIRS // count, 0),
    )
    return rows, pl.BlockSpec((MEMBERS, 2, count, 16, C), lambda n: (0, 0, n, 0, 0))


def pack_kernel(x_ref, cot_ref, out_ref, wide):
    count = x_ref.shape[2]
    for which, ref in enumerate((x_ref, cot_ref)):
        for side in range(2):
            lanes = slice(side * 128, side * 128 + 128)
            for row in range(OWN_ROWS):
                wide[which, side, pl.ds(row, count, stride=OWN_ROWS), :] = ref[0, row, :, lanes].astype(F32)
            for pair in range(count // SIDE):
                own = wide[which, side, pair * SIDE * OWN_ROWS : (pair + 1) * SIDE * OWN_ROWS]
                out_ref[:, which, pair, :, lanes] = own.reshape(MEMBERS, 16, 128).astype(BF16)


def pack(alignment, cotangent, first, pairs, count):
    rows, packed = pair_specs(first, count)
    return pl.pallas_call(
        pack_kernel,
        grid=(pairs // count,),
        in_specs=[rows, rows],
        out_specs=packed,
        out_shape=pltpu.HBM((MEMBERS, 2, pairs, 16, C), BF16),
        scratch_shapes=[pltpu.VMEM((2, 2, count * SIDE * OWN_ROWS, 128), F32)],
        compiler_params=pltpu.CompilerParams(vmem_limit_bytes=VMEM),
        cost_estimate=pl.CostEstimate(flops=0, bytes_accessed=pairs * 2**19, transcendentals=0),
    )(alignment, cotangent)


def unpack_kernel(*refs):
    in_ref, upd_ref, grad_ref, wide = refs[0], *refs[-3:]
    count = upd_ref.shape[2]
    for which, ref in enumerate((upd_ref, grad_ref)):
        for side in range(2):
            lanes = slice(side * 128, side * 128 + 128)
            for pair in range(count // SIDE):
                wide[which, side, pair * SIDE * OWN_ROWS : (pair + 1) * SIDE * OWN_ROWS] = (
                    in_ref[:, which, pair, :, lanes].astype(F32).reshape(SIDE * OWN_ROWS, 128)
                )
            for row in range(OWN_ROWS):
                ref[0, row, :, lanes] = wide[
                    which, side, pl.ds(row, count, stride=OWN_ROWS), :
                ].astype(BF16)


def unpack(packed, first, structs, earlier, count):
    rows, blocks = pair_specs(first, count)
    shape = pltpu.HBM((structs, OWN_ROWS, RES, C), BF16)
    return pl.pallas_call(
        unpack_kernel,
        grid=(packed.shape[2] // count,),
        in_specs=[blocks] + [pl.BlockSpec(memory_space=pl.ANY)] * len(earlier),
        out_specs=[rows, rows],
        out_shape=[shape, shape],
        input_output_aliases={1 + k: k for k in range(len(earlier))},
        scratch_shapes=[pltpu.VMEM((2, 2, count * SIDE * OWN_ROWS, 128), F32)],
        compiler_params=pltpu.CompilerParams(vmem_limit_bytes=24 * 2**20),
        cost_estimate=pl.CostEstimate(
            flops=0, bytes_accessed=packed.shape[2] * 2**19, transcendentals=0
        ),
    )(packed, *earlier)


def token_rows(block):
    wide = block.astype(F32)
    return jnp.concatenate(
        [
            wide[:, pair, side : side + 8].reshape(ROWS, C)
            for pair in range(block.shape[1])
            for side in (0, 8)
        ],
        axis=0,
    )


def row_blocks(tokens, pair):
    first = tokens[2 * pair * ROWS : (2 * pair + 1) * ROWS].reshape(MEMBERS, 8, C)
    other = tokens[(2 * pair + 1) * ROWS : (2 * pair + 2) * ROWS].reshape(MEMBERS, 8, C)
    return jnp.concatenate([first, other], axis=1)


def fold_rows(tokens):
    return jnp.sum(tokens.reshape(tokens.shape[0] // 8, 8, C), axis=0)


def tiles_of(matrix):
    count = matrix.shape[0] // 8
    return matrix[:, :128].reshape(count, 8, 128), matrix[:, 128:].reshape(count, 8, 128)


def pair_kernel(steps, has_earlier, last, *refs):
    core_ref, x_ref, cot_ref, w_ref, wt_ref, wo_ref, gb_ref, rows_ref = refs[:8]
    qc, kc, vc, dac, attc, dprojc, gin, gout, vec, dlog = refs[-10:]
    if last:
        own_ref, other_ref, sums_ref = refs[-13:-10]
        out_refs = refs[-14:-13]
    else:
        sums_ref = refs[-11]
        out_refs = refs[-11 - steps : -11]

    @pl.when(pl.program_id(0) == 0)
    def _():
        gin[...] = jnp.zeros_like(gin)
        gout[...] = jnp.zeros_like(gout)
        vec[...] = jnp.zeros_like(vec)
        dlog[...] = jnp.zeros_like(dlog)

    pairs = x_ref.shape[2]
    out_bias, gain, bias = rows_ref[0:1], rows_ref[1:2], rows_ref[2:3]
    x = token_rows(x_ref[:, 0])
    cot = token_rows(cot_ref[:, 0])
    cot_half = cot.astype(BF16)
    centered = x - jnp.mean(x, axis=-1, keepdims=True)
    inv_std = lax.rsqrt(jnp.mean(centered * centered, axis=-1, keepdims=True) + EPSILON)
    standard = centered * inv_std
    normed = (standard * gain + bias).astype(BF16)

    kv = dot(normed, w_ref[:, HD : 3 * HD]).astype(BF16)
    proj = dot(wt_ref[...], normed, 1, 1)
    qc[...] = (proj[:HD] * INV_SCALE).astype(BF16)
    kc[...] = proj[HD : 2 * HD].astype(BF16)
    vc[...] = proj[2 * HD : 3 * HD].astype(BF16)
    gate = jax.nn.sigmoid(proj[3 * HD :] + jnp.concatenate([gb_ref[...]] * (2 * pairs), axis=1))
    d_gated = dot(wo_ref[...], cot_half, 1, 1)
    dac[...] = (d_gated * gate).astype(BF16)

    head_of_lane = lax.broadcasted_iota(jnp.int32, (1, 128), 1) // HDIM
    for r in range(2 * pairs):
        toks = slice(r * ROWS, (r + 1) * ROWS)
        for half in range(2):
            lanes = slice(half * 128, half * 128 + 128)
            k_half = kv[toks, half * 128 : half * 128 + 128]
            v_half = kv[toks, HD + half * 128 : HD + half * 128 + 128]
            zero = jnp.zeros_like(k_half)
            k_stack = jnp.concatenate(
                [jnp.where(head_of_lane == h, k_half, zero) for h in range(4)], axis=0
            )
            v_stack = jnp.concatenate(
                [jnp.where(head_of_lane == h, v_half, zero) for h in range(4)], axis=0
            )
            scores = dot(k_stack, qc[lanes, toks])
            d_softs = dot(v_stack, dac[lanes, toks])
            for hp in range(2):
                probs, d_ss = [], []
                for h in (2 * hp, 2 * hp + 1):
                    s = scores[h * 128 : h * 128 + 128]
                    d_soft = d_softs[h * 128 : h * 128 + 128]
                    shifted = jnp.exp(s - jnp.max(s, axis=0, keepdims=True))
                    soft = shifted * (1.0 / jnp.sum(shifted, axis=0, keepdims=True))
                    weighted = soft * d_soft
                    d_s = (weighted - soft * jnp.sum(weighted, axis=0, keepdims=True)).astype(BF16)
                    probs.append(soft.astype(BF16))
                    d_ss.append(d_s)
                probs = jnp.concatenate(probs, axis=0)
                d_ss = jnp.concatenate(d_ss, axis=0)
                f = half * 128 + hp * 2 * HDIM
                chans = slice(f, f + 2 * HDIM)
                hole = jnp.zeros((HDIM, ROWS), BF16)

                def diagonal(rows):
                    return jnp.concatenate(
                        [
                            jnp.concatenate([rows[:HDIM], hole], axis=1),
                            jnp.concatenate([hole, rows[HDIM:]], axis=1),
                        ],
                        axis=0,
                    )

                def blocks(wide):
                    return jnp.concatenate([wide[:HDIM, :ROWS], wide[HDIM:, ROWS:]], axis=0)

                attc[chans, toks] = dot(diagonal(vc[chans, toks]), probs)
                dprojc[chans, toks] = (dot(diagonal(kc[chans, toks]), d_ss) * INV_SCALE).astype(BF16)
                dprojc[HD + f : HD + f + 2 * HDIM, toks] = blocks(dot(qc[chans, toks], d_ss, 1, 1)).astype(BF16)
                dprojc[2 * HD + f : 2 * HD + f + 2 * HDIM, toks] = blocks(
                    dot(dac[chans, toks], probs, 1, 1)
                ).astype(BF16)


    gated = gate * attc[...]
    d_logit = (d_gated * gated * (1.0 - gate)).astype(BF16)
    dprojc[3 * HD :, :] = d_logit
    gated_half = gated.astype(BF16)
    wide_logit = d_logit.astype(F32)
    dlog[...] += functools.reduce(
        jnp.add, [wide_logit[:, r * ROWS : (r + 1) * ROWS] for r in range(2 * pairs)]
    )
    gin[...] += dot(dprojc[...], normed)
    gout[...] += dot(gated_half, cot_half)
    update = dot(gated_half.T, wo_ref[...]) + out_bias
    updated = x + update
    d_normed = dot(w_ref[...], dprojc[...]).T
    d_hat = d_normed * gain
    d_std = d_normed * standard
    branch = inv_std * (
        d_hat
        - jnp.mean(d_hat, axis=-1, keepdims=True)
        - standard * jnp.mean(d_hat * standard, axis=-1, keepdims=True)
    )
    grad = cot + branch

    def store(ref):
        for pair in range(pairs):
            ref[:, 0, pair] = row_blocks(updated, pair).astype(BF16)
            ref[:, 1, pair] = row_blocks(grad, pair).astype(BF16)

    if last:
        store(out_refs[0])
    else:
        for step, ref in enumerate(out_refs):
            pl.when(pl.program_id(0) == step)(functools.partial(store, ref))
    vec[0] += fold_rows(cot)
    vec[1] += fold_rows(d_std)
    vec[2] += fold_rows(d_normed)

    @pl.when(pl.program_id(0) == steps - 1)
    def _():
        def put(half, first, tiles):
            count = tiles.shape[0]
            if has_earlier:
                tiles = tiles + refs[8][half, first : first + count]
            sums_ref[half, first : first + count] = tiles

        for block in range(5):
            matrix = gin[block * HD : (block + 1) * HD].T if block < 4 else gout[...]
            for half, tiles in enumerate(tiles_of(matrix)):
                put(half, block * 32, tiles)
        rows = [jnp.sum(dlog[...].T, axis=0, keepdims=True)] + [
            jnp.sum(vec[k], axis=0, keepdims=True) for k in range(3)
        ]
        vectors = [row[:, side : side + 128] for row in rows for side in (0, 128)]
        put(0, 160, jnp.concatenate(vectors, axis=0)[None])
        sums_ref[0, 161:] = jnp.zeros((TILES - 161, 8, 128), F32)
        sums_ref[1, 160:] = jnp.zeros((TILES - 160, 8, 128), F32)
        if last:
            core = core_ref[0]
            own_ref[...] = sums_ref[core]
            other_ref[...] = sums_ref[1 - core]


def columns(packed, core, params, sums=None, last=False):
    pairs = packed.shape[2] // STEPS

    def part(which):
        return pl.BlockSpec((MEMBERS, 1, pairs, 16, C), lambda p: (0, which, p, 0, 0))

    def whole(shape):
        return pl.BlockSpec(shape, lambda p: (0,) * len(shape))

    half = (TILES, 8, 128)
    operands = [core, packed, packed, *params]
    in_specs = [pl.BlockSpec(memory_space=pltpu.SMEM), part(0), part(1)] + [whole(a.shape) for a in params]
    if sums is not None:
        operands.append(sums)
        in_specs.append(whole(sums.shape))
    wide = (HD, 2 * pairs * ROWS)
    scratch = [pltpu.VMEM(wide, BF16)] * 4 + [
        pltpu.VMEM(wide, F32),
        pltpu.VMEM((4 * HD, 2 * pairs * ROWS), BF16),
        pltpu.VMEM((4 * HD, C), F32),
        pltpu.VMEM((HD, C), F32),
        pltpu.VMEM((3, 8, C), F32),
        pltpu.VMEM((HD, 128), F32),
    ]
    if last:
        out_specs = [pl.BlockSpec((MEMBERS, 2, pairs, 16, C), lambda p: (0, 0, p, 0, 0))]
        out_shape = [pltpu.HBM(packed.shape, BF16)]
        out_specs += [whole(half)] * 2
        out_shape += [pltpu.HBM(half, F32)] * 2
        scratch.insert(0, pltpu.VMEM((2, *half), F32))
    else:
        out_specs = [whole((MEMBERS, 2, pairs, 16, C))] * STEPS + [whole((2, *half))]
        out_shape = [pltpu.HBM((MEMBERS, 2, pairs, 16, C), BF16)] * STEPS
        out_shape.append(pltpu.HBM((2, *half), F32))
    return pl.pallas_call(
        functools.partial(pair_kernel, STEPS, sums is not None, last),
        grid=(STEPS,),
        in_specs=in_specs,
        out_specs=out_specs,
        out_shape=out_shape,
        scratch_shapes=scratch,
        compiler_params=pltpu.CompilerParams(
            dimension_semantics=("arbitrary",), vmem_limit_bytes=VMEM
        ),
        cost_estimate=pl.CostEstimate(
            flops=packed.shape[2] * 4_000_000_000, bytes_accessed=2**23, transcendentals=packed.shape[2] * 300_000
        ),
    )(*operands)


def shift(value, axes, size, step):
    return lax.ppermute(value, axes, [(k, (k + step) % size) for k in range(size)])


def scatter_sum(terms, axes, size):
    own = lax.axis_index(axes)
    count = terms[0].shape[0] // size

    def block_for(step):
        place = lax.rem(own + step, size) * count
        return functools.reduce(
            jnp.add, [lax.dynamic_slice_in_dim(term, place, count, 0) for term in terms]
        )

    arrived = [shift(block_for(step), axes, size, step) for step in range(1, size)]
    return functools.reduce(jnp.add, arrived, block_for(0))


def gather(value, axes, size):
    own = lax.axis_index(axes)
    count = value.shape[0]
    arrived = [shift(value, axes, size, step) for step in range(1, size)]
    total = jnp.zeros((size * count, *value.shape[1:]), value.dtype)
    for step, piece in enumerate([value, *arrived]):
        place = lax.rem(own + size - step, size) * count
        total = lax.dynamic_update_slice_in_dim(total, piece, place, 0)
    return total


def swap(value, axis):
    return lax.ppermute(value, axis, [(0, 1), (1, 0)])


def meet_sum(value, axes, size):
    own = lax.axis_index(axes)
    arrived = [shift(value, axes, size, step) for step in range(1, size)]
    met = jnp.concatenate([value, *arrived], axis=0).reshape(size, *value.shape)
    pieces = [
        lax.dynamic_index_in_dim(met, lax.rem(own + size - k, size), 0, keepdims=False)
        for k in range(size)
    ]
    return functools.reduce(jnp.add, pieces)


def finish_kernel(core_ref, own_ref, other_ref, mats_ref, out_ref, vec_ref):
    def write(halves):
        for half, ref in enumerate(halves):
            lanes = slice(half * 128, half * 128 + 128)
            for block in range(4):
                mats_ref[block, :, lanes] = ref[block * 32 : block * 32 + 32].reshape(C, 128)
            out_ref[:, lanes] = ref[128:160].reshape(C, 128)
        for k in range(8):
            vec_ref[k // 2 : k // 2 + 1, k % 2 * 128 : k % 2 * 128 + 128] = halves[0][160, k : k + 1]

    pl.when(core_ref[0] == 0)(lambda: write((own_ref, other_ref)))
    pl.when(core_ref[0] == 1)(lambda: write((other_ref, own_ref)))


def finish(core, own, other):
    vmem = pl.BlockSpec(memory_space=pltpu.VMEM)
    return pl.pallas_call(
        finish_kernel,
        in_specs=[pl.BlockSpec(memory_space=pltpu.SMEM), vmem, vmem],
        out_specs=[vmem] * 3,
        out_shape=[
            jax.ShapeDtypeStruct((4, C, HD), F32),
            jax.ShapeDtypeStruct((HD, C), F32),
            jax.ShapeDtypeStruct((4, C), F32),
        ],
        compiler_params=pltpu.CompilerParams(vmem_limit_bytes=16 * 2**20),
        cost_estimate=pl.CostEstimate(flops=0, bytes_accessed=2**22, transcendentals=0),
    )(core, own, other)


def rows_sum(own, other):
    tiles = scatter_sum([own, swap(other, "core")], "y", 4)
    return scatter_sum([tiles], "x", 4)


def shards(alignment, cotangent, wq, wk, wv, wg, gate_bias, wo, out_bias, gain, bias):
    structs = alignment.shape[0]
    w = jnp.concatenate([wq, wk, wv, wg], axis=1)
    rows = jnp.concatenate([jnp.stack([out_bias, gain, bias]), jnp.zeros((5, C), F32)], axis=0)
    params = (w, w.T, wo, jnp.broadcast_to(gate_bias[:, None], (HD, 128)), rows)
    core = lax.axis_index("core").reshape(1)
    after = lax.optimization_barrier

    def exchange(value):
        return lax.all_to_all(value, DAP, 0, 0, tiled=True)

    first = exchange(pack(alignment, cotangent, 0, 10, 2))
    second = exchange(pack(alignment, cotangent, 10, 6, 2))
    early, middle, sums = columns(first, core, params)
    early = exchange(early)
    late, own, other = columns(second, core, params, sums, last=True)
    middle = exchange(middle)
    tiles, late = after((meet_sum(rows_sum(own, other), RING, 8) * FACTOR, late))
    late = exchange(late)
    done = unpack(early, 0, structs, (), 1)
    done = unpack(middle, 5, structs, tuple(done), 1)
    for axis in ("x", "y"):
        tiles = gather(tiles, axis, 4)
    mats, out, vectors = finish(core, tiles, swap(tiles, "core"))
    return (*unpack(late, 10, structs, tuple(done), 2), mats, out, vectors)


def solution(mesh):
    parts = Mesh(mesh.devices.reshape(2, 4, 2, 4, 4), BATCH + DAP)
    split = P(BATCH, DAP, None, None)
    return jax.shard_map(
        shards,
        mesh=parts,
        in_specs=(split, split) + (P(),) * 9,
        out_specs=(split, split, P(), P(), P()),
        check_vma=False,
    )
```

```python
import functools
import math

import jax
import jax.numpy as jnp
from jax import lax
from jax.experimental import pallas as pl
from jax.experimental.pallas import tpu as pltpu
from jax.sharding import Mesh
from jax.sharding import PartitionSpec as P

C = 256
HEADS = 8
HDIM = 32
ROWS = 128
RES = 256
HD = 256
STRUCTS = 32
EPSILON = 1e-05
INV_SCALE = 1.0 / math.sqrt(HDIM)
FACTOR = 1.0 / math.sqrt(STRUCTS * ROWS * RES)
F32 = jnp.float32
BF16 = jnp.bfloat16

MEMBERS = 16
OWN_ROWS = ROWS // MEMBERS
SIDE = 2 * MEMBERS
PAIRS = RES // SIDE
DAP = ("z_lo", "x")
BATCH = ("z_hi", "y", "core")
RING = ("z_hi", "z_lo")
TILES = 176
VMEM = 60 * 2**20


def dot(left, right, left_dim=1, right_dim=0):
    return lax.dot_general(
        left, right, (((left_dim,), (right_dim,)), ((), ())), preferred_element_type=F32
    )


def pair_specs(first, count):
    rows = pl.BlockSpec(
        (1, OWN_ROWS, count * SIDE, C),
        lambda n: ((first + n * count) // PAIRS, 0, (first + n * count) % PAIRS // count, 0),
    )
    return rows, pl.BlockSpec((MEMBERS, 2, count, 16, C), lambda n: (0, 0, n, 0, 0))


def pack_kernel(x_ref, cot_ref, out_ref, wide):
    count = x_ref.shape[2]
    for which, ref in enumerate((x_ref, cot_ref)):
        for side in range(2):
            lanes = slice(side * 128, side * 128 + 128)
            for row in range(OWN_ROWS):
                wide[which, side, pl.ds(row, count, stride=OWN_ROWS), :] = ref[0, row, :, lanes].astype(F32)
            for pair in range(count // SIDE):
                own = wide[which, side, pair * SIDE * OWN_ROWS : (pair + 1) * SIDE * OWN_ROWS]
                out_ref[:, which, pair, :, lanes] = own.reshape(MEMBERS, 16, 128).astype(BF16)


def pack(alignment, cotangent, first, pairs, count):
    rows, packed = pair_specs(first, count)
    return pl.pallas_call(
        pack_kernel,
        grid=(pairs // count,),
        in_specs=[rows, rows],
        out_specs=packed,
        out_shape=pltpu.HBM((MEMBERS, 2, pairs, 16, C), BF16),
        scratch_shapes=[pltpu.VMEM((2, 2, count * SIDE * OWN_ROWS, 128), F32)],
        compiler_params=pltpu.CompilerParams(vmem_limit_bytes=VMEM),
        cost_estimate=pl.CostEstimate(flops=0, bytes_accessed=pairs * 2**19, transcendentals=0),
    )(alignment, cotangent)


def unpack_kernel(*refs):
    in_ref, upd_ref, grad_ref, wide = refs[0], *refs[-3:]
    count = upd_ref.shape[2]
    for which, ref in enumerate((upd_ref, grad_ref)):
        for side in range(2):
            lanes = slice(side * 128, side * 128 + 128)
            for pair in range(count // SIDE):
                wide[which, side, pair * SIDE * OWN_ROWS : (pair + 1) * SIDE * OWN_ROWS] = (
                    in_ref[:, which, pair, :, lanes].astype(F32).reshape(SIDE * OWN_ROWS, 128)
                )
            for row in range(OWN_ROWS):
                ref[0, row, :, lanes] = wide[
                    which, side, pl.ds(row, count, stride=OWN_ROWS), :
                ].astype(BF16)


def unpack(packed, first, structs, earlier, count):
    rows, blocks = pair_specs(first, count)
    shape = pltpu.HBM((structs, OWN_ROWS, RES, C), BF16)
    return pl.pallas_call(
        unpack_kernel,
        grid=(packed.shape[2] // count,),
        in_specs=[blocks] + [pl.BlockSpec(memory_space=pl.ANY)] * len(earlier),
        out_specs=[rows, rows],
        out_shape=[shape, shape],
        input_output_aliases={1 + k: k for k in range(len(earlier))},
        scratch_shapes=[pltpu.VMEM((2, 2, count * SIDE * OWN_ROWS, 128), F32)],
        compiler_params=pltpu.CompilerParams(vmem_limit_bytes=24 * 2**20),
        cost_estimate=pl.CostEstimate(
            flops=0, bytes_accessed=packed.shape[2] * 2**19, transcendentals=0
        ),
    )(packed, *earlier)


def token_rows(block):
    wide = block.astype(F32)
    return jnp.concatenate(
        [
            wide[:, pair, side : side + 8].reshape(ROWS, C)
            for pair in range(block.shape[1])
            for side in (0, 8)
        ],
        axis=0,
    )


def row_blocks(tokens, pair):
    first = tokens[2 * pair * ROWS : (2 * pair + 1) * ROWS].reshape(MEMBERS, 8, C)
    other = tokens[(2 * pair + 1) * ROWS : (2 * pair + 2) * ROWS].reshape(MEMBERS, 8, C)
    return jnp.concatenate([first, other], axis=1)


def fold_rows(tokens):
    return jnp.sum(tokens.reshape(tokens.shape[0] // 8, 8, C), axis=0)


def tiles_of(matrix):
    count = matrix.shape[0] // 8
    return matrix[:, :128].reshape(count, 8, 128), matrix[:, 128:].reshape(count, 8, 128)


def pair_kernel(steps, has_earlier, last, *refs):
    core_ref, x_ref, cot_ref, w_ref, wt_ref, wo_ref, gb_ref, rows_ref = refs[:8]
    qc, kc, vc, dac, attc, dprojc, gin, gout, vec, dlog = refs[-10:]
    if last:
        own_ref, other_ref, sums_ref = refs[-13:-10]
        out_refs = refs[-14:-13]
    else:
        sums_ref = refs[-11]
        out_refs = refs[-13:-11]

    @pl.when(pl.program_id(0) == 0)
    def _():
        gin[...] = jnp.zeros_like(gin)
        gout[...] = jnp.zeros_like(gout)
        vec[...] = jnp.zeros_like(vec)
        dlog[...] = jnp.zeros_like(dlog)

    pairs = x_ref.shape[2]
    out_bias, gain, bias = rows_ref[0:1], rows_ref[1:2], rows_ref[2:3]
    x = token_rows(x_ref[:, 0])
    cot = token_rows(cot_ref[:, 0])
    cot_half = cot.astype(BF16)
    centered = x - jnp.mean(x, axis=-1, keepdims=True)
    inv_std = lax.rsqrt(jnp.mean(centered * centered, axis=-1, keepdims=True) + EPSILON)
    standard = centered * inv_std
    normed = (standard * gain + bias).astype(BF16)

    kv = dot(normed, w_ref[:, HD : 3 * HD]).astype(BF16)
    proj = dot(wt_ref[...], normed, 1, 1)
    qc[...] = (proj[:HD] * INV_SCALE).astype(BF16)
    kc[...] = proj[HD : 2 * HD].astype(BF16)
    vc[...] = proj[2 * HD : 3 * HD].astype(BF16)
    gate = jax.nn.sigmoid(proj[3 * HD :] + jnp.concatenate([gb_ref[...]] * (2 * pairs), axis=1))
    d_gated = dot(wo_ref[...], cot_half, 1, 1)
    dac[...] = (d_gated * gate).astype(BF16)

    head_of_lane = lax.broadcasted_iota(jnp.int32, (1, 128), 1) // HDIM
    for r in range(2 * pairs):
        toks = slice(r * ROWS, (r + 1) * ROWS)
        for half in range(2):
            lanes = slice(half * 128, half * 128 + 128)
            k_half = kv[toks, half * 128 : half * 128 + 128]
            v_half = kv[toks, HD + half * 128 : HD + half * 128 + 128]
            zero = jnp.zeros_like(k_half)
            k_stack = jnp.concatenate(
                [jnp.where(head_of_lane == h, k_half, zero) for h in range(4)], axis=0
            )
            v_stack = jnp.concatenate(
                [jnp.where(head_of_lane == h, v_half, zero) for h in range(4)], axis=0
            )
            scores = dot(k_stack, qc[lanes, toks])
            d_softs = dot(v_stack, dac[lanes, toks])
            for hp in range(2):
                probs, d_ss = [], []
                for h in (2 * hp, 2 * hp + 1):
                    s = scores[h * 128 : h * 128 + 128]
                    d_soft = d_softs[h * 128 : h * 128 + 128]
                    shifted = jnp.exp(s - jnp.max(s, axis=0, keepdims=True))
                    soft = shifted * (1.0 / jnp.sum(shifted, axis=0, keepdims=True))
                    weighted = soft * d_soft
                    d_s = (weighted - soft * jnp.sum(weighted, axis=0, keepdims=True)).astype(BF16)
                    probs.append(soft.astype(BF16))
                    d_ss.append(d_s)
                probs = jnp.concatenate(probs, axis=0)
                d_ss = jnp.concatenate(d_ss, axis=0)
                f = half * 128 + hp * 2 * HDIM
                chans = slice(f, f + 2 * HDIM)
                hole = jnp.zeros((HDIM, ROWS), BF16)

                def diagonal(rows):
                    return jnp.concatenate(
                        [
                            jnp.concatenate([rows[:HDIM], hole], axis=1),
                            jnp.concatenate([hole, rows[HDIM:]], axis=1),
                        ],
                        axis=0,
                    )

                def blocks(wide):
                    return jnp.concatenate([wide[:HDIM, :ROWS], wide[HDIM:, ROWS:]], axis=0)

                attc[chans, toks] = dot(diagonal(vc[chans, toks]), probs)
                dprojc[chans, toks] = (dot(diagonal(kc[chans, toks]), d_ss) * INV_SCALE).astype(BF16)
                dprojc[HD + f : HD + f + 2 * HDIM, toks] = blocks(dot(qc[chans, toks], d_ss, 1, 1)).astype(BF16)
                dprojc[2 * HD + f : 2 * HD + f + 2 * HDIM, toks] = blocks(
                    dot(dac[chans, toks], probs, 1, 1)
                ).astype(BF16)


    gated = gate * attc[...]
    d_logit = (d_gated * gated * (1.0 - gate)).astype(BF16)
    dprojc[3 * HD :, :] = d_logit
    gated_half = gated.astype(BF16)
    wide_logit = d_logit.astype(F32)
    dlog[...] += functools.reduce(
        jnp.add, [wide_logit[:, r * ROWS : (r + 1) * ROWS] for r in range(2 * pairs)]
    )
    gin[...] += dot(dprojc[...], normed)
    gout[...] += dot(gated_half, cot_half)
    update = dot(gated_half.T, wo_ref[...]) + out_bias
    updated = x + update
    d_normed = dot(w_ref[...], dprojc[...]).T
    d_hat = d_normed * gain
    d_std = d_normed * standard
    branch = inv_std * (
        d_hat
        - jnp.mean(d_hat, axis=-1, keepdims=True)
        - standard * jnp.mean(d_hat * standard, axis=-1, keepdims=True)
    )
    grad = cot + branch

    def store(ref):
        for pair in range(pairs):
            ref[:, 0, pair] = row_blocks(updated, pair).astype(BF16)
            ref[:, 1, pair] = row_blocks(grad, pair).astype(BF16)

    if last:
        store(out_refs[0])
    else:
        more = pl.program_id(0) < steps - 1
        pl.when(more)(lambda: store(out_refs[0]))
        pl.when(jnp.logical_not(more))(lambda: store(out_refs[1]))
    vec[0] += fold_rows(cot)
    vec[1] += fold_rows(d_std)
    vec[2] += fold_rows(d_normed)

    @pl.when(pl.program_id(0) == steps - 1)
    def _():
        def put(half, first, tiles):
            count = tiles.shape[0]
            if has_earlier:
                tiles = tiles + refs[8][half, first : first + count]
            sums_ref[half, first : first + count] = tiles

        for block in range(5):
            matrix = gin[block * HD : (block + 1) * HD].T if block < 4 else gout[...]
            for half, tiles in enumerate(tiles_of(matrix)):
                put(half, block * 32, tiles)
        rows = [jnp.sum(dlog[...].T, axis=0, keepdims=True)] + [
            jnp.sum(vec[k], axis=0, keepdims=True) for k in range(3)
        ]
        vectors = [row[:, side : side + 128] for row in rows for side in (0, 128)]
        put(0, 160, jnp.concatenate(vectors, axis=0)[None])
        sums_ref[0, 161:] = jnp.zeros((TILES - 161, 8, 128), F32)
        sums_ref[1, 160:] = jnp.zeros((TILES - 160, 8, 128), F32)
        if last:
            core = core_ref[0]
            own_ref[...] = sums_ref[core]
            other_ref[...] = sums_ref[1 - core]


def columns(packed, core, params, pairs, sums=None, last=False):
    steps = packed.shape[2] // pairs

    def part(which):
        return pl.BlockSpec((MEMBERS, 1, pairs, 16, C), lambda p: (0, which, p, 0, 0))

    def whole(shape):
        return pl.BlockSpec(shape, lambda p: (0,) * len(shape))

    half = (TILES, 8, 128)
    operands = [core, packed, packed, *params]
    in_specs = [pl.BlockSpec(memory_space=pltpu.SMEM), part(0), part(1)] + [whole(a.shape) for a in params]
    if sums is not None:
        operands.append(sums)
        in_specs.append(whole(sums.shape))
    wide = (HD, 2 * pairs * ROWS)
    scratch = [pltpu.VMEM(wide, BF16)] * 4 + [
        pltpu.VMEM(wide, F32),
        pltpu.VMEM((4 * HD, 2 * pairs * ROWS), BF16),
        pltpu.VMEM((4 * HD, C), F32),
        pltpu.VMEM((HD, C), F32),
        pltpu.VMEM((3, 8, C), F32),
        pltpu.VMEM((HD, 128), F32),
    ]
    if last:
        out_specs = [pl.BlockSpec((MEMBERS, 2, pairs, 16, C), lambda p: (0, 0, p, 0, 0))]
        out_shape = [pltpu.HBM(packed.shape, BF16)]
        out_specs += [whole(half)] * 2
        out_shape += [pltpu.HBM(half, F32)] * 2
        scratch.insert(0, pltpu.VMEM((2, *half), F32))
    else:
        block = (MEMBERS, 2, pairs, 16, C)
        most = pl.BlockSpec(block, lambda p: (0, 0, jnp.minimum(p, steps - 2), 0, 0))
        out_specs = [most, whole(block), whole((2, *half))]
        out_shape = [pltpu.HBM((MEMBERS, 2, (steps - 1) * pairs, 16, C), BF16), pltpu.HBM(block, BF16)]
        out_shape.append(pltpu.HBM((2, *half), F32))
    return pl.pallas_call(
        functools.partial(pair_kernel, steps, sums is not None, last),
        grid=(steps,),
        in_specs=in_specs,
        out_specs=out_specs,
        out_shape=out_shape,
        scratch_shapes=scratch,
        compiler_params=pltpu.CompilerParams(
            dimension_semantics=("arbitrary",), vmem_limit_bytes=VMEM
        ),
        cost_estimate=pl.CostEstimate(
            flops=packed.shape[2] * 4_000_000_000, bytes_accessed=2**23, transcendentals=packed.shape[2] * 300_000
        ),
    )(*operands)


def shift(value, axes, size, step):
    return lax.ppermute(value, axes, [(k, (k + step) % size) for k in range(size)])


def scatter_sum(terms, axes, size):
    own = lax.axis_index(axes)
    count = terms[0].shape[0] // size

    def block_for(step):
        place = lax.rem(own + step, size) * count
        return functools.reduce(
            jnp.add, [lax.dynamic_slice_in_dim(term, place, count, 0) for term in terms]
        )

    arrived = [shift(block_for(step), axes, size, step) for step in range(1, size)]
    return functools.reduce(jnp.add, arrived, block_for(0))


def gather(value, axes, size):
    own = lax.axis_index(axes)
    count = value.shape[0]
    arrived = [shift(value, axes, size, step) for step in range(1, size)]
    total = jnp.zeros((size * count, *value.shape[1:]), value.dtype)
    for step, piece in enumerate([value, *arrived]):
        place = lax.rem(own + size - step, size) * count
        total = lax.dynamic_update_slice_in_dim(total, piece, place, 0)
    return total


def swap(value, axis):
    return lax.ppermute(value, axis, [(0, 1), (1, 0)])


def meet_sum(value, axes, size):
    own = lax.axis_index(axes)
    arrived = [shift(value, axes, size, step) for step in range(1, size)]
    met = jnp.concatenate([value, *arrived], axis=0).reshape(size, *value.shape)
    pieces = [
        lax.dynamic_index_in_dim(met, lax.rem(own + size - k, size), 0, keepdims=False)
        for k in range(size)
    ]
    return functools.reduce(jnp.add, pieces)


def finish_kernel(core_ref, own_ref, other_ref, mats_ref, out_ref, vec_ref):
    def write(halves):
        for half, ref in enumerate(halves):
            lanes = slice(half * 128, half * 128 + 128)
            for block in range(4):
                mats_ref[block, :, lanes] = ref[block * 32 : block * 32 + 32].reshape(C, 128)
            out_ref[:, lanes] = ref[128:160].reshape(C, 128)
        for k in range(8):
            vec_ref[k // 2 : k // 2 + 1, k % 2 * 128 : k % 2 * 128 + 128] = halves[0][160, k : k + 1]

    pl.when(core_ref[0] == 0)(lambda: write((own_ref, other_ref)))
    pl.when(core_ref[0] == 1)(lambda: write((other_ref, own_ref)))


def finish(core, own, other):
    vmem = pl.BlockSpec(memory_space=pltpu.VMEM)
    return pl.pallas_call(
        finish_kernel,
        in_specs=[pl.BlockSpec(memory_space=pltpu.SMEM), vmem, vmem],
        out_specs=[vmem] * 3,
        out_shape=[
            jax.ShapeDtypeStruct((4, C, HD), F32),
            jax.ShapeDtypeStruct((HD, C), F32),
            jax.ShapeDtypeStruct((4, C), F32),
        ],
        compiler_params=pltpu.CompilerParams(vmem_limit_bytes=16 * 2**20),
        cost_estimate=pl.CostEstimate(flops=0, bytes_accessed=2**22, transcendentals=0),
    )(core, own, other)


def rows_sum(own, other):
    tiles = scatter_sum([own, swap(other, "core")], "y", 4)
    return scatter_sum([tiles], "x", 4)


def shards(alignment, cotangent, wq, wk, wv, wg, gate_bias, wo, out_bias, gain, bias):
    structs = alignment.shape[0]
    w = jnp.concatenate([wq, wk, wv, wg], axis=1)
    rows = jnp.concatenate([jnp.stack([out_bias, gain, bias]), jnp.zeros((5, C), F32)], axis=0)
    params = (w, w.T, wo, jnp.broadcast_to(gate_bias[:, None], (HD, 128)), rows)
    core = lax.axis_index("core").reshape(1)
    after = lax.optimization_barrier

    def exchange(value):
        return lax.all_to_all(value, DAP, 0, 0, tiled=True)

    first = exchange(pack(alignment, cotangent, 0, 10, 2))
    second = exchange(pack(alignment, cotangent, 10, 6, 2))
    early, middle, sums = columns(first, core, params, 2)
    early = exchange(early)
    late, own, other = columns(second, core, params, 3, sums, last=True)
    tiles, middle, early = after((rows_sum(own, other), middle, early))
    middle = exchange(middle)
    tiles, late = after((meet_sum(tiles, RING, 8) * FACTOR, late))
    late = exchange(late)
    done = unpack(early, 0, structs, (), 2)
    done = unpack(middle, 8, structs, tuple(done), 2)
    for axis in ("x", "y"):
        tiles = gather(tiles, axis, 4)
    mats, out, vectors = finish(core, tiles, swap(tiles, "core"))
    return (*unpack(late, 10, structs, tuple(done), 2), mats, out, vectors)


def solution(mesh):
    parts = Mesh(mesh.devices.reshape(2, 4, 2, 4, 4), BATCH + DAP)
    split = P(BATCH, DAP, None, None)
    return jax.shard_map(
        shards,
        mesh=parts,
        in_specs=(split, split) + (P(),) * 9,
        out_specs=(split, split, P(), P(), P()),
        check_vma=False,
    )
```

```python
import functools
import math

import jax
import jax.numpy as jnp
from jax import lax
from jax.experimental import pallas as pl
from jax.experimental.pallas import tpu as pltpu
from jax.sharding import Mesh
from jax.sharding import PartitionSpec as P

C = 256
HEADS = 8
HDIM = 32
ROWS = 128
RES = 256
HD = 256
STRUCTS = 32
EPSILON = 1e-05
INV_SCALE = 1.0 / math.sqrt(HDIM)
FACTOR = 1.0 / math.sqrt(STRUCTS * ROWS * RES)
F32 = jnp.float32
BF16 = jnp.bfloat16

MEMBERS = 16
OWN_ROWS = ROWS // MEMBERS
UNITS = 4
PAIRS = 2
STEPS = 2
DAP = ("z_lo", "x")
BATCH = ("z_hi", "y", "core")
RING = ("z_hi", "z_lo")
TILES = 176
GROUP = 16
COUNT = GROUP * 2 * PAIRS
VMEM = 60 * 2**20


def dot(left, right, left_dim=1, right_dim=0):
    return lax.dot_general(
        left, right, (((left_dim,), (right_dim,)), ((), ())), preferred_element_type=F32
    )


def unit_specs(first):
    rows = pl.BlockSpec(
        (1, OWN_ROWS, COUNT, C),
        lambda n, g: ((first + n) // UNITS, 0, (first + n) % UNITS * (MEMBERS // GROUP) + g, 0),
    )
    packed = pl.BlockSpec((GROUP, 2, PAIRS, 16, C), lambda n, g: (g, 0, n, 0, 0))
    return rows, packed


def pack_kernel(x_ref, cot_ref, out_ref, wide):
    for which, ref in enumerate((x_ref, cot_ref)):
        for side in range(2):
            lanes = slice(side * 128, side * 128 + 128)
            for row in range(OWN_ROWS):
                wide[which, side, pl.ds(row, COUNT, stride=OWN_ROWS), :] = ref[0, row, :, lanes].astype(F32)
            out_ref[:, which, :, :, lanes] = wide[which, side].reshape(GROUP, PAIRS, 16, 128).astype(BF16)


def pack(alignment, cotangent, first, units):
    rows, packed = unit_specs(first)
    return pl.pallas_call(
        pack_kernel,
        grid=(units, MEMBERS // GROUP),
        in_specs=[rows, rows],
        out_specs=packed,
        out_shape=pltpu.HBM((MEMBERS, 2, units * PAIRS, 16, C), BF16),
        scratch_shapes=[pltpu.VMEM((2, 2, COUNT * OWN_ROWS, 128), F32)],
        compiler_params=pltpu.CompilerParams(vmem_limit_bytes=VMEM),
        cost_estimate=pl.CostEstimate(flops=0, bytes_accessed=units * 2**21, transcendentals=0),
    )(alignment, cotangent)


def unpack_kernel(*refs):
    in_ref, upd_ref, grad_ref, wide = refs[0], *refs[-3:]
    for which, ref in enumerate((upd_ref, grad_ref)):
        for side in range(2):
            lanes = slice(side * 128, side * 128 + 128)
            wide[which, side] = in_ref[:, which, :, :, lanes].astype(F32).reshape(COUNT * OWN_ROWS, 128)
            for row in range(OWN_ROWS):
                ref[0, row, :, lanes] = wide[
                    which, side, pl.ds(row, COUNT, stride=OWN_ROWS), :
                ].astype(BF16)


def unpack(packed, first, structs, earlier):
    rows, blocks = unit_specs(first)
    shape = pltpu.HBM((structs, OWN_ROWS, RES, C), BF16)
    units = packed.shape[2] // PAIRS
    return pl.pallas_call(
        unpack_kernel,
        grid=(units, MEMBERS // GROUP),
        in_specs=[blocks] + [pl.BlockSpec(memory_space=pl.ANY)] * len(earlier),
        out_specs=[rows, rows],
        out_shape=[shape, shape],
        input_output_aliases={1 + k: k for k in range(len(earlier))},
        scratch_shapes=[pltpu.VMEM((2, 2, COUNT * OWN_ROWS, 128), F32)],
        compiler_params=pltpu.CompilerParams(vmem_limit_bytes=24 * 2**20),
        cost_estimate=pl.CostEstimate(flops=0, bytes_accessed=units * 2**21, transcendentals=0),
    )(packed, *earlier)


def token_rows(block):
    wide = block.astype(F32)
    return jnp.concatenate(
        [
            wide[:, pair, side : side + 8].reshape(ROWS, C)
            for pair in range(block.shape[1])
            for side in (0, 8)
        ],
        axis=0,
    )


def row_blocks(tokens, pair):
    first = tokens[2 * pair * ROWS : (2 * pair + 1) * ROWS].reshape(MEMBERS, 8, C)
    other = tokens[(2 * pair + 1) * ROWS : (2 * pair + 2) * ROWS].reshape(MEMBERS, 8, C)
    return jnp.concatenate([first, other], axis=1)


def fold_rows(tokens):
    return jnp.sum(tokens.reshape(tokens.shape[0] // 8, 8, C), axis=0)


def tiles_of(matrix):
    count = matrix.shape[0] // 8
    return matrix[:, :128].reshape(count, 8, 128), matrix[:, 128:].reshape(count, 8, 128)


def pair_kernel(steps, has_earlier, last, *refs):
    core_ref, x_ref, cot_ref, w_ref, wt_ref, wo_ref, gb_ref, rows_ref = refs[:8]
    qc, kc, vc, dac, attc, dprojc, gin, gout, vec, dlog = refs[-10:]
    if last:
        out_ref, own_ref, other_ref, sums_ref, refs = *refs[-14:-10], refs[:-10]
    else:
        out_ref, sums_ref = refs[-12:-10]

    @pl.when(pl.program_id(0) == 0)
    def _():
        gin[...] = jnp.zeros_like(gin)
        gout[...] = jnp.zeros_like(gout)
        vec[...] = jnp.zeros_like(vec)
        dlog[...] = jnp.zeros_like(dlog)

    pairs = x_ref.shape[2]
    out_bias, gain, bias = rows_ref[0:1], rows_ref[1:2], rows_ref[2:3]
    x = token_rows(x_ref[:, 0])
    cot = token_rows(cot_ref[:, 0])
    cot_half = cot.astype(BF16)
    centered = x - jnp.mean(x, axis=-1, keepdims=True)
    inv_std = lax.rsqrt(jnp.mean(centered * centered, axis=-1, keepdims=True) + EPSILON)
    standard = centered * inv_std
    normed = (standard * gain + bias).astype(BF16)

    kv = dot(normed, w_ref[:, HD : 3 * HD]).astype(BF16)
    proj = dot(wt_ref[...], normed, 1, 1)
    qc[...] = (proj[:HD] * INV_SCALE).astype(BF16)
    kc[...] = proj[HD : 2 * HD].astype(BF16)
    vc[...] = proj[2 * HD : 3 * HD].astype(BF16)
    gate = jax.nn.sigmoid(proj[3 * HD :] + jnp.concatenate([gb_ref[...]] * (2 * pairs), axis=1))
    d_gated = dot(wo_ref[...], cot_half, 1, 1)
    dac[...] = (d_gated * gate).astype(BF16)

    head_of_lane = lax.broadcasted_iota(jnp.int32, (1, 128), 1) // HDIM
    for r in range(2 * pairs):
        toks = slice(r * ROWS, (r + 1) * ROWS)
        for half in range(2):
            lanes = slice(half * 128, half * 128 + 128)
            k_half = kv[toks, half * 128 : half * 128 + 128]
            v_half = kv[toks, HD + half * 128 : HD + half * 128 + 128]
            zero = jnp.zeros_like(k_half)
            k_stack = jnp.concatenate(
                [jnp.where(head_of_lane == h, k_half, zero) for h in range(4)], axis=0
            )
            v_stack = jnp.concatenate(
                [jnp.where(head_of_lane == h, v_half, zero) for h in range(4)], axis=0
            )
            scores = dot(k_stack, qc[lanes, toks])
            d_softs = dot(v_stack, dac[lanes, toks])
            for hp in range(2):
                probs, d_ss = [], []
                for h in (2 * hp, 2 * hp + 1):
                    s = scores[h * 128 : h * 128 + 128]
                    d_soft = d_softs[h * 128 : h * 128 + 128]
                    shifted = jnp.exp(s - jnp.max(s, axis=0, keepdims=True))
                    soft = shifted * (1.0 / jnp.sum(shifted, axis=0, keepdims=True))
                    weighted = soft * d_soft
                    d_s = (weighted - soft * jnp.sum(weighted, axis=0, keepdims=True)).astype(BF16)
                    probs.append(soft.astype(BF16))
                    d_ss.append(d_s)
                probs = jnp.concatenate(probs, axis=0)
                d_ss = jnp.concatenate(d_ss, axis=0)
                f = half * 128 + hp * 2 * HDIM
                chans = slice(f, f + 2 * HDIM)
                hole = jnp.zeros((HDIM, ROWS), BF16)

                def diagonal(rows):
                    return jnp.concatenate(
                        [
                            jnp.concatenate([rows[:HDIM], hole], axis=1),
                            jnp.concatenate([hole, rows[HDIM:]], axis=1),
                        ],
                        axis=0,
                    )

                def blocks(wide):
                    return jnp.concatenate([wide[:HDIM, :ROWS], wide[HDIM:, ROWS:]], axis=0)

                attc[chans, toks] = dot(diagonal(vc[chans, toks]), probs)
                dprojc[chans, toks] = (dot(diagonal(kc[chans, toks]), d_ss) * INV_SCALE).astype(BF16)
                dprojc[HD + f : HD + f + 2 * HDIM, toks] = blocks(dot(qc[chans, toks], d_ss, 1, 1)).astype(BF16)
                dprojc[2 * HD + f : 2 * HD + f + 2 * HDIM, toks] = blocks(
                    dot(dac[chans, toks], probs, 1, 1)
                ).astype(BF16)


    gated = gate * attc[...]
    d_logit = (d_gated * gated * (1.0 - gate)).astype(BF16)
    dprojc[3 * HD :, :] = d_logit
    gated_half = gated.astype(BF16)
    wide_logit = d_logit.astype(F32)
    dlog[...] += functools.reduce(
        jnp.add, [wide_logit[:, r * ROWS : (r + 1) * ROWS] for r in range(2 * pairs)]
    )
    gin[...] += dot(dprojc[...], normed)
    gout[...] += dot(gated_half, cot_half)
    update = dot(gated_half.T, wo_ref[...]) + out_bias
    updated = x + update
    d_normed = dot(w_ref[...], dprojc[...]).T
    d_hat = d_normed * gain
    d_std = d_normed * standard
    branch = inv_std * (
        d_hat
        - jnp.mean(d_hat, axis=-1, keepdims=True)
        - standard * jnp.mean(d_hat * standard, axis=-1, keepdims=True)
    )
    grad = cot + branch
    for pair in range(pairs):
        out_ref[:, 0, pair] = row_blocks(updated, pair).astype(BF16)
        out_ref[:, 1, pair] = row_blocks(grad, pair).astype(BF16)
    vec[0] += fold_rows(cot)
    vec[1] += fold_rows(d_std)
    vec[2] += fold_rows(d_normed)

    @pl.when(pl.program_id(0) == steps - 1)
    def _():
        def put(half, first, tiles):
            count = tiles.shape[0]
            if has_earlier:
                tiles = tiles + refs[8][half, first : first + count]
            sums_ref[half, first : first + count] = tiles

        for block in range(5):
            matrix = gin[block * HD : (block + 1) * HD].T if block < 4 else gout[...]
            for half, tiles in enumerate(tiles_of(matrix)):
                put(half, block * 32, tiles)
        rows = [jnp.sum(dlog[...].T, axis=0, keepdims=True)] + [
            jnp.sum(vec[k], axis=0, keepdims=True) for k in range(3)
        ]
        vectors = [row[:, side : side + 128] for row in rows for side in (0, 128)]
        put(0, 160, jnp.concatenate(vectors, axis=0)[None])
        sums_ref[0, 161:] = jnp.zeros((TILES - 161, 8, 128), F32)
        sums_ref[1, 160:] = jnp.zeros((TILES - 160, 8, 128), F32)
        if last:
            core = core_ref[0]
            own_ref[...] = sums_ref[core]
            other_ref[...] = sums_ref[1 - core]


def columns(packed, core, params, sums=None, last=False):
    pairs = packed.shape[2] // STEPS

    def part(which):
        return pl.BlockSpec((MEMBERS, 1, pairs, 16, C), lambda p: (0, which, p, 0, 0))

    def whole(shape):
        return pl.BlockSpec(shape, lambda p: (0,) * len(shape))

    half = (TILES, 8, 128)
    operands = [core, packed, packed, *params]
    in_specs = [pl.BlockSpec(memory_space=pltpu.SMEM), part(0), part(1)] + [whole(a.shape) for a in params]
    if sums is not None:
        operands.append(sums)
        in_specs.append(whole(sums.shape))
    out_specs = [pl.BlockSpec((MEMBERS, 2, pairs, 16, C), lambda p: (0, 0, p, 0, 0))]
    out_shape = [pltpu.HBM(packed.shape, BF16)]
    wide = (HD, 2 * pairs * ROWS)
    scratch = [pltpu.VMEM(wide, BF16)] * 4 + [
        pltpu.VMEM(wide, F32),
        pltpu.VMEM((4 * HD, 2 * pairs * ROWS), BF16),
        pltpu.VMEM((4 * HD, C), F32),
        pltpu.VMEM((HD, C), F32),
        pltpu.VMEM((3, 8, C), F32),
        pltpu.VMEM((HD, 128), F32),
    ]
    if last:
        out_specs += [whole(half)] * 2
        out_shape += [pltpu.HBM(half, F32)] * 2
        scratch.insert(0, pltpu.VMEM((2, *half), F32))
    else:
        out_specs.append(whole((2, *half)))
        out_shape.append(pltpu.HBM((2, *half), F32))
    return pl.pallas_call(
        functools.partial(pair_kernel, STEPS, sums is not None, last),
        grid=(STEPS,),
        in_specs=in_specs,
        out_specs=out_specs,
        out_shape=out_shape,
        scratch_shapes=scratch,
        compiler_params=pltpu.CompilerParams(
            dimension_semantics=("arbitrary",), vmem_limit_bytes=VMEM
        ),
        cost_estimate=pl.CostEstimate(
            flops=packed.shape[2] * 4_000_000_000, bytes_accessed=2**23, transcendentals=packed.shape[2] * 300_000
        ),
    )(*operands)


def shift(value, axes, size, step):
    return lax.ppermute(value, axes, [(k, (k + step) % size) for k in range(size)])


def scatter_sum(terms, axes, size):
    own = lax.axis_index(axes)
    count = terms[0].shape[0] // size

    def block_for(step):
        place = lax.rem(own + step, size) * count
        return functools.reduce(
            jnp.add, [lax.dynamic_slice_in_dim(term, place, count, 0) for term in terms]
        )

    arrived = [shift(block_for(step), axes, size, step) for step in range(1, size)]
    return functools.reduce(jnp.add, arrived, block_for(0))


def gather(value, axes, size):
    own = lax.axis_index(axes)
    count = value.shape[0]
    arrived = [shift(value, axes, size, step) for step in range(1, size)]
    total = jnp.zeros((size * count, *value.shape[1:]), value.dtype)
    for step, piece in enumerate([value, *arrived]):
        place = lax.rem(own + size - step, size) * count
        total = lax.dynamic_update_slice_in_dim(total, piece, place, 0)
    return total


def swap(value, axis):
    return lax.ppermute(value, axis, [(0, 1), (1, 0)])


def meet_sum(value, axes, size):
    own = lax.axis_index(axes)
    arrived = [shift(value, axes, size, step) for step in range(1, size)]
    met = jnp.concatenate([value, *arrived], axis=0).reshape(size, *value.shape)
    pieces = [
        lax.dynamic_index_in_dim(met, lax.rem(own + size - k, size), 0, keepdims=False)
        for k in range(size)
    ]
    return functools.reduce(jnp.add, pieces)


def finish_kernel(core_ref, own_ref, other_ref, mats_ref, out_ref, vec_ref):
    def write(halves):
        for half, ref in enumerate(halves):
            lanes = slice(half * 128, half * 128 + 128)
            for block in range(4):
                mats_ref[block, :, lanes] = ref[block * 32 : block * 32 + 32].reshape(C, 128)
            out_ref[:, lanes] = ref[128:160].reshape(C, 128)
        for k in range(8):
            vec_ref[k // 2 : k // 2 + 1, k % 2 * 128 : k % 2 * 128 + 128] = halves[0][160, k : k + 1]

    pl.when(core_ref[0] == 0)(lambda: write((own_ref, other_ref)))
    pl.when(core_ref[0] == 1)(lambda: write((other_ref, own_ref)))


def finish(core, own, other):
    vmem = pl.BlockSpec(memory_space=pltpu.VMEM)
    return pl.pallas_call(
        finish_kernel,
        in_specs=[pl.BlockSpec(memory_space=pltpu.SMEM), vmem, vmem],
        out_specs=[vmem] * 3,
        out_shape=[
            jax.ShapeDtypeStruct((4, C, HD), F32),
            jax.ShapeDtypeStruct((HD, C), F32),
            jax.ShapeDtypeStruct((4, C), F32),
        ],
        compiler_params=pltpu.CompilerParams(vmem_limit_bytes=16 * 2**20),
        cost_estimate=pl.CostEstimate(flops=0, bytes_accessed=2**22, transcendentals=0),
    )(core, own, other)


def rows_sum(own, other):
    tiles = scatter_sum([own, swap(other, "core")], "y", 4)
    return scatter_sum([tiles], "x", 4)


def shards(alignment, cotangent, wq, wk, wv, wg, gate_bias, wo, out_bias, gain, bias):
    structs = alignment.shape[0]
    w = jnp.concatenate([wq, wk, wv, wg], axis=1)
    rows = jnp.concatenate([jnp.stack([out_bias, gain, bias]), jnp.zeros((5, C), F32)], axis=0)
    params = (w, w.T, wo, jnp.broadcast_to(gate_bias[:, None], (HD, 128)), rows)
    core = lax.axis_index("core").reshape(1)
    after = lax.optimization_barrier

    def exchange(value):
        return lax.all_to_all(value, DAP, 0, 0, tiled=True)

    first = exchange(pack(alignment, cotangent, 0, 5))
    second = exchange(pack(alignment, cotangent, 5, 3))
    early, sums = columns(first, core, params)
    early = exchange(early)
    late, own, other = columns(second, core, params, sums, last=True)
    tiles = rows_sum(own, other)
    tiles = (tiles + swap(tiles, "z_hi")) * FACTOR
    tiles, late = after((meet_sum(tiles, "z_lo", 4), late))
    late = exchange(late)
    done = unpack(early, 0, structs, ())
    for axis in ("x", "y"):
        tiles = gather(tiles, axis, 4)
    mats, out, vectors = finish(core, tiles, swap(tiles, "core"))
    return (*unpack(late, 5, structs, tuple(done)), mats, out, vectors)


def solution(mesh):
    parts = Mesh(mesh.devices.reshape(2, 4, 2, 4, 4), BATCH + DAP)
    split = P(BATCH, DAP, None, None)
    return jax.shard_map(
        shards,
        mesh=parts,
        in_specs=(split, split) + (P(),) * 9,
        out_specs=(split, split, P(), P(), P()),
        check_vma=False,
    )
```

```python
import functools
import math

import jax
import jax.numpy as jnp
from jax import lax
from jax.experimental import pallas as pl
from jax.experimental.pallas import tpu as pltpu
from jax.sharding import Mesh
from jax.sharding import PartitionSpec as P

C = 256
HEADS = 8
HDIM = 32
ROWS = 128
RES = 256
HD = 256
STRUCTS = 32
EPSILON = 1e-05
INV_SCALE = 1.0 / math.sqrt(HDIM)
FACTOR = 1.0 / math.sqrt(STRUCTS * ROWS * RES)
F32 = jnp.float32
BF16 = jnp.bfloat16

MEMBERS = 16
OWN_ROWS = ROWS // MEMBERS
UNITS = 4
PAIRS = 2
DAP = ("z_lo", "x")
BATCH = ("z_hi", "y", "core")
RING = ("z_hi", "z_lo")
TILES = 176
COUNT = MEMBERS * 2 * PAIRS
VMEM = 60 * 2**20


def dot(left, right, left_dim=1, right_dim=0):
    return lax.dot_general(
        left, right, (((left_dim,), (right_dim,)), ((), ())), preferred_element_type=F32
    )


def rows_of(ref, unit):
    return ref.at[unit // UNITS, :, pl.ds(unit % UNITS * COUNT, COUNT), :]


def pack_kernel(first, units, x_ref, cot_ref, out_ref, held, made, in_sems, out_sems):
    def arrival(n, which):
        source = rows_of((x_ref, cot_ref)[which], first + n)
        return pltpu.make_async_copy(source, held.at[n, which], in_sems.at[n, which])

    def departure(n):
        target = out_ref.at[:, :, pl.ds(n * PAIRS, PAIRS), :, :]
        return pltpu.make_async_copy(made.at[n], target, out_sems.at[n])

    for n in range(units):
        for which in range(2):
            arrival(n, which).start()
    for n in range(units):
        for which in range(2):
            arrival(n, which).wait()
            turned = jnp.swapaxes(held[n, which], 0, 1)
            made[n, :, which] = turned.reshape(MEMBERS, PAIRS, 16, C)
        departure(n).start()
    for n in range(units):
        departure(n).wait()


def pack(alignment, cotangent, first, units):
    anywhere = pl.BlockSpec(memory_space=pl.ANY)
    return pl.pallas_call(
        functools.partial(pack_kernel, first, units),
        in_specs=[anywhere, anywhere],
        out_specs=anywhere,
        out_shape=pltpu.HBM((MEMBERS, 2, units * PAIRS, 16, C), BF16),
        scratch_shapes=[
            pltpu.VMEM((units, 2, OWN_ROWS, COUNT, C), BF16),
            pltpu.VMEM((units, MEMBERS, 2, PAIRS, 16, C), BF16),
            pltpu.SemaphoreType.DMA((units, 2)),
            pltpu.SemaphoreType.DMA((units,)),
        ],
        compiler_params=pltpu.CompilerParams(vmem_limit_bytes=VMEM),
        cost_estimate=pl.CostEstimate(flops=0, bytes_accessed=units * 2**20, transcendentals=0),
    )(alignment, cotangent)


def unpack_kernel(first, units, *refs):
    in_ref, upd_ref, grad_ref, held, made, in_sems, out_sems = refs[0], *refs[-6:]

    def arrival(n):
        source = in_ref.at[:, :, pl.ds(n * PAIRS, PAIRS), :, :]
        return pltpu.make_async_copy(source, held.at[n], in_sems.at[n])

    def departure(n, which):
        target = rows_of((upd_ref, grad_ref)[which], first + n)
        return pltpu.make_async_copy(made.at[n, which], target, out_sems.at[n, which])

    for n in range(units):
        arrival(n).start()
    for n in range(units):
        arrival(n).wait()
        for which in range(2):
            turned = held[n, :, which].reshape(COUNT, OWN_ROWS, C)
            made[n, which] = jnp.swapaxes(turned, 0, 1)
            departure(n, which).start()
    for n in range(units):
        for which in range(2):
            departure(n, which).wait()


def unpack(packed, first, structs, earlier):
    anywhere = pl.BlockSpec(memory_space=pl.ANY)
    shape = pltpu.HBM((structs, OWN_ROWS, RES, C), BF16)
    units = packed.shape[2] // PAIRS
    return pl.pallas_call(
        functools.partial(unpack_kernel, first, units),
        in_specs=[anywhere] * (1 + len(earlier)),
        out_specs=[anywhere, anywhere],
        out_shape=[shape, shape],
        input_output_aliases={1 + k: k for k in range(len(earlier))},
        scratch_shapes=[
            pltpu.VMEM((units, MEMBERS, 2, PAIRS, 16, C), BF16),
            pltpu.VMEM((units, 2, OWN_ROWS, COUNT, C), BF16),
            pltpu.SemaphoreType.DMA((units,)),
            pltpu.SemaphoreType.DMA((units, 2)),
        ],
        compiler_params=pltpu.CompilerParams(vmem_limit_bytes=24 * 2**20),
        cost_estimate=pl.CostEstimate(flops=0, bytes_accessed=units * 2**20, transcendentals=0),
    )(packed, *earlier)


def token_rows(block):
    wide = block.astype(F32)
    return jnp.concatenate(
        [
            wide[:, pair, side : side + 8].reshape(ROWS, C)
            for pair in range(block.shape[1])
            for side in (0, 8)
        ],
        axis=0,
    )


def row_blocks(tokens, pair):
    first = tokens[2 * pair * ROWS : (2 * pair + 1) * ROWS].reshape(MEMBERS, 8, C)
    other = tokens[(2 * pair + 1) * ROWS : (2 * pair + 2) * ROWS].reshape(MEMBERS, 8, C)
    return jnp.concatenate([first, other], axis=1)


def fold_rows(tokens):
    return jnp.sum(tokens.reshape(tokens.shape[0] // 8, 8, C), axis=0)


def tiles_of(matrix):
    count = matrix.shape[0] // 8
    return matrix[:, :128].reshape(count, 8, 128), matrix[:, 128:].reshape(count, 8, 128)


def pair_kernel(steps, has_earlier, last, *refs):
    core_ref, x_ref, cot_ref, w_ref, wt_ref, wo_ref, gb_ref, rows_ref = refs[:8]
    qc, kc, vc, dac, attc, dprojc, gin, gout, vec, dlog = refs[-10:]
    if last:
        out_ref, own_ref, other_ref, sums_ref, refs = *refs[-14:-10], refs[:-10]
    else:
        out_ref, sums_ref = refs[-12:-10]

    @pl.when(pl.program_id(0) == 0)
    def _():
        gin[...] = jnp.zeros_like(gin)
        gout[...] = jnp.zeros_like(gout)
        vec[...] = jnp.zeros_like(vec)
        dlog[...] = jnp.zeros_like(dlog)

    pairs = x_ref.shape[2]
    out_bias, gain, bias = rows_ref[0:1], rows_ref[1:2], rows_ref[2:3]
    x = token_rows(x_ref[:, 0])
    cot = token_rows(cot_ref[:, 0])
    cot_half = cot.astype(BF16)
    centered = x - jnp.mean(x, axis=-1, keepdims=True)
    inv_std = lax.rsqrt(jnp.mean(centered * centered, axis=-1, keepdims=True) + EPSILON)
    standard = centered * inv_std
    normed = (standard * gain + bias).astype(BF16)

    kv = dot(normed, w_ref[:, HD : 3 * HD]).astype(BF16)
    proj = dot(wt_ref[...], normed, 1, 1)
    qc[...] = (proj[:HD] * INV_SCALE).astype(BF16)
    kc[...] = proj[HD : 2 * HD].astype(BF16)
    vc[...] = proj[2 * HD : 3 * HD].astype(BF16)
    gate = jax.nn.sigmoid(proj[3 * HD :] + jnp.concatenate([gb_ref[...]] * (2 * pairs), axis=1))
    d_gated = dot(wo_ref[...], cot_half, 1, 1)
    dac[...] = (d_gated * gate).astype(BF16)

    head_of_lane = lax.broadcasted_iota(jnp.int32, (1, 128), 1) // HDIM
    for r in range(2 * pairs):
        toks = slice(r * ROWS, (r + 1) * ROWS)
        for half in range(2):
            lanes = slice(half * 128, half * 128 + 128)
            k_half = kv[toks, half * 128 : half * 128 + 128]
            v_half = kv[toks, HD + half * 128 : HD + half * 128 + 128]
            zero = jnp.zeros_like(k_half)
            k_stack = jnp.concatenate(
                [jnp.where(head_of_lane == h, k_half, zero) for h in range(4)], axis=0
            )
            v_stack = jnp.concatenate(
                [jnp.where(head_of_lane == h, v_half, zero) for h in range(4)], axis=0
            )
            scores = dot(k_stack, qc[lanes, toks])
            d_softs = dot(v_stack, dac[lanes, toks])
            for hp in range(2):
                probs, d_ss = [], []
                for h in (2 * hp, 2 * hp + 1):
                    s = scores[h * 128 : h * 128 + 128]
                    d_soft = d_softs[h * 128 : h * 128 + 128]
                    shifted = jnp.exp(s - jnp.max(s, axis=0, keepdims=True))
                    soft = shifted * (1.0 / jnp.sum(shifted, axis=0, keepdims=True))
                    weighted = soft * d_soft
                    d_s = (weighted - soft * jnp.sum(weighted, axis=0, keepdims=True)).astype(BF16)
                    probs.append(soft.astype(BF16))
                    d_ss.append(d_s)
                probs = jnp.concatenate(probs, axis=0)
                d_ss = jnp.concatenate(d_ss, axis=0)
                f = half * 128 + hp * 2 * HDIM
                chans = slice(f, f + 2 * HDIM)
                hole = jnp.zeros((HDIM, ROWS), BF16)

                def diagonal(rows):
                    return jnp.concatenate(
                        [
                            jnp.concatenate([rows[:HDIM], hole], axis=1),
                            jnp.concatenate([hole, rows[HDIM:]], axis=1),
                        ],
                        axis=0,
                    )

                def blocks(wide):
                    return jnp.concatenate([wide[:HDIM, :ROWS], wide[HDIM:, ROWS:]], axis=0)

                attc[chans, toks] = dot(diagonal(vc[chans, toks]), probs)
                dprojc[chans, toks] = (dot(diagonal(kc[chans, toks]), d_ss) * INV_SCALE).astype(BF16)
                dprojc[HD + f : HD + f + 2 * HDIM, toks] = blocks(dot(qc[chans, toks], d_ss, 1, 1)).astype(BF16)
                dprojc[2 * HD + f : 2 * HD + f + 2 * HDIM, toks] = blocks(
                    dot(dac[chans, toks], probs, 1, 1)
                ).astype(BF16)


    gated = gate * attc[...]
    d_logit = (d_gated * gated * (1.0 - gate)).astype(BF16)
    dprojc[3 * HD :, :] = d_logit
    gated_half = gated.astype(BF16)
    wide_logit = d_logit.astype(F32)
    dlog[...] += functools.reduce(
        jnp.add, [wide_logit[:, r * ROWS : (r + 1) * ROWS] for r in range(2 * pairs)]
    )
    gin[...] += dot(dprojc[...], normed)
    gout[...] += dot(gated_half, cot_half)
    update = dot(gated_half.T, wo_ref[...]) + out_bias
    updated = x + update
    d_normed = dot(w_ref[...], dprojc[...]).T
    d_hat = d_normed * gain
    d_std = d_normed * standard
    branch = inv_std * (
        d_hat
        - jnp.mean(d_hat, axis=-1, keepdims=True)
        - standard * jnp.mean(d_hat * standard, axis=-1, keepdims=True)
    )
    grad = cot + branch
    for pair in range(pairs):
        out_ref[:, 0, pair] = row_blocks(updated, pair).astype(BF16)
        out_ref[:, 1, pair] = row_blocks(grad, pair).astype(BF16)
    vec[0] += fold_rows(cot)
    vec[1] += fold_rows(d_std)
    vec[2] += fold_rows(d_normed)

    @pl.when(pl.program_id(0) == steps - 1)
    def _():
        def put(half, first, tiles):
            count = tiles.shape[0]
            if has_earlier:
                tiles = tiles + refs[8][half, first : first + count]
            sums_ref[half, first : first + count] = tiles

        for block in range(5):
            matrix = gin[block * HD : (block + 1) * HD].T if block < 4 else gout[...]
            for half, tiles in enumerate(tiles_of(matrix)):
                put(half, block * 32, tiles)
        rows = [jnp.sum(dlog[...].T, axis=0, keepdims=True)] + [
            jnp.sum(vec[k], axis=0, keepdims=True) for k in range(3)
        ]
        vectors = [row[:, side : side + 128] for row in rows for side in (0, 128)]
        put(0, 160, jnp.concatenate(vectors, axis=0)[None])
        sums_ref[0, 161:] = jnp.zeros((TILES - 161, 8, 128), F32)
        sums_ref[1, 160:] = jnp.zeros((TILES - 160, 8, 128), F32)
        if last:
            core = core_ref[0]
            own_ref[...] = sums_ref[core]
            other_ref[...] = sums_ref[1 - core]


def columns(packed, core, params, steps, sums=None, last=False):
    pairs = packed.shape[2] // steps

    def part(which):
        return pl.BlockSpec((MEMBERS, 1, pairs, 16, C), lambda p: (0, which, p, 0, 0))

    def whole(shape):
        return pl.BlockSpec(shape, lambda p: (0,) * len(shape))

    half = (TILES, 8, 128)
    operands = [core, packed, packed, *params]
    in_specs = [pl.BlockSpec(memory_space=pltpu.SMEM), part(0), part(1)] + [whole(a.shape) for a in params]
    if sums is not None:
        operands.append(sums)
        in_specs.append(whole(sums.shape))
    out_specs = [pl.BlockSpec((MEMBERS, 2, pairs, 16, C), lambda p: (0, 0, p, 0, 0))]
    out_shape = [pltpu.HBM(packed.shape, BF16)]
    wide = (HD, 2 * pairs * ROWS)
    scratch = [pltpu.VMEM(wide, BF16)] * 4 + [
        pltpu.VMEM(wide, F32),
        pltpu.VMEM((4 * HD, 2 * pairs * ROWS), BF16),
        pltpu.VMEM((4 * HD, C), F32),
        pltpu.VMEM((HD, C), F32),
        pltpu.VMEM((3, 8, C), F32),
        pltpu.VMEM((HD, 128), F32),
    ]
    if last:
        out_specs += [whole(half)] * 2
        out_shape += [pltpu.HBM(half, F32)] * 2
        scratch.insert(0, pltpu.VMEM((2, *half), F32))
    else:
        out_specs.append(whole((2, *half)))
        out_shape.append(pltpu.HBM((2, *half), F32))
    return pl.pallas_call(
        functools.partial(pair_kernel, steps, sums is not None, last),
        grid=(steps,),
        in_specs=in_specs,
        out_specs=out_specs,
        out_shape=out_shape,
        scratch_shapes=scratch,
        compiler_params=pltpu.CompilerParams(
            dimension_semantics=("arbitrary",), vmem_limit_bytes=VMEM
        ),
        cost_estimate=pl.CostEstimate(
            flops=packed.shape[2] * 4_000_000_000, bytes_accessed=2**23, transcendentals=packed.shape[2] * 300_000
        ),
    )(*operands)


def shift(value, axes, size, step):
    return lax.ppermute(value, axes, [(k, (k + step) % size) for k in range(size)])


def scatter_sum(terms, axes, size):
    own = lax.axis_index(axes)
    count = terms[0].shape[0] // size

    def block_for(step):
        place = lax.rem(own + step, size) * count
        return functools.reduce(
            jnp.add, [lax.dynamic_slice_in_dim(term, place, count, 0) for term in terms]
        )

    arrived = [shift(block_for(step), axes, size, step) for step in range(1, size)]
    return functools.reduce(jnp.add, arrived, block_for(0))


def gather(value, axes, size):
    own = lax.axis_index(axes)
    count = value.shape[0]
    arrived = [shift(value, axes, size, step) for step in range(1, size)]
    total = jnp.zeros((size * count, *value.shape[1:]), value.dtype)
    for step, piece in enumerate([value, *arrived]):
        place = lax.rem(own + size - step, size) * count
        total = lax.dynamic_update_slice_in_dim(total, piece, place, 0)
    return total


def swap(value, axis):
    return lax.ppermute(value, axis, [(0, 1), (1, 0)])


def meet_sum(value, axes, size):
    own = lax.axis_index(axes)
    arrived = [shift(value, axes, size, step) for step in range(1, size)]
    met = jnp.concatenate([value, *arrived], axis=0).reshape(size, *value.shape)
    pieces = [
        lax.dynamic_index_in_dim(met, lax.rem(own + size - k, size), 0, keepdims=False)
        for k in range(size)
    ]
    return functools.reduce(jnp.add, pieces)


def finish_kernel(core_ref, own_ref, other_ref, mats_ref, out_ref, vec_ref):
    def write(halves):
        for half, ref in enumerate(halves):
            lanes = slice(half * 128, half * 128 + 128)
            for block in range(4):
                mats_ref[block, :, lanes] = ref[block * 32 : block * 32 + 32].reshape(C, 128)
            out_ref[:, lanes] = ref[128:160].reshape(C, 128)
        for k in range(8):
            vec_ref[k // 2 : k // 2 + 1, k % 2 * 128 : k % 2 * 128 + 128] = halves[0][160, k : k + 1]

    pl.when(core_ref[0] == 0)(lambda: write((own_ref, other_ref)))
    pl.when(core_ref[0] == 1)(lambda: write((other_ref, own_ref)))


def finish(core, own, other):
    vmem = pl.BlockSpec(memory_space=pltpu.VMEM)
    return pl.pallas_call(
        finish_kernel,
        in_specs=[pl.BlockSpec(memory_space=pltpu.SMEM), vmem, vmem],
        out_specs=[vmem] * 3,
        out_shape=[
            jax.ShapeDtypeStruct((4, C, HD), F32),
            jax.ShapeDtypeStruct((HD, C), F32),
            jax.ShapeDtypeStruct((4, C), F32),
        ],
        compiler_params=pltpu.CompilerParams(vmem_limit_bytes=16 * 2**20),
        cost_estimate=pl.CostEstimate(flops=0, bytes_accessed=2**22, transcendentals=0),
    )(core, own, other)


def rows_sum(own, other):
    tiles = scatter_sum([own, swap(other, "core")], "y", 4)
    return scatter_sum([tiles], "x", 4)


def shards(alignment, cotangent, wq, wk, wv, wg, gate_bias, wo, out_bias, gain, bias):
    structs = alignment.shape[0]
    w = jnp.concatenate([wq, wk, wv, wg], axis=1)
    rows = jnp.concatenate([jnp.stack([out_bias, gain, bias]), jnp.zeros((5, C), F32)], axis=0)
    params = (w, w.T, wo, jnp.broadcast_to(gate_bias[:, None], (HD, 128)), rows)
    core = lax.axis_index("core").reshape(1)
    after = lax.optimization_barrier

    def exchange(value):
        return lax.all_to_all(value, DAP, 0, 0, tiled=True)

    first = exchange(pack(alignment, cotangent, 0, 5))
    second = exchange(pack(alignment, cotangent, 5, 3))
    early, sums = columns(first, core, params, 2)
    early = exchange(early)
    late, own, other = columns(second, core, params, 1, sums, last=True)
    tiles = rows_sum(own, other)
    tiles = (tiles + swap(tiles, "z_hi")) * FACTOR
    tiles, late = after((meet_sum(tiles, "z_lo", 4), late))
    late = exchange(late)
    done = unpack(early, 0, structs, ())
    for axis in ("x", "y"):
        tiles = gather(tiles, axis, 4)
    mats, out, vectors = finish(core, tiles, swap(tiles, "core"))
    return (*unpack(late, 5, structs, tuple(done)), mats, out, vectors)


def solution(mesh):
    parts = Mesh(mesh.devices.reshape(2, 4, 2, 4, 4), BATCH + DAP)
    split = P(BATCH, DAP, None, None)
    return jax.shard_map(
        shards,
        mesh=parts,
        in_specs=(split, split) + (P(),) * 9,
        out_specs=(split, split, P(), P(), P()),
        check_vma=False,
    )
```

```python
import functools
import math

import jax
import jax.numpy as jnp
from jax import lax
from jax.experimental import pallas as pl
from jax.experimental.pallas import tpu as pltpu
from jax.sharding import Mesh
from jax.sharding import PartitionSpec as P

C = 256
HEADS = 8
HDIM = 32
ROWS = 128
RES = 256
HD = 256
STRUCTS = 32
EPSILON = 1e-05
INV_SCALE = 1.0 / math.sqrt(HDIM)
FACTOR = 1.0 / math.sqrt(STRUCTS * ROWS * RES)
F32 = jnp.float32
BF16 = jnp.bfloat16

MEMBERS = 16
OWN_ROWS = ROWS // MEMBERS
UNITS = 4
PAIRS = 2
DAP = ("z_lo", "x")
BATCH = ("z_hi", "y", "core")
RING = ("z_hi", "z_lo")
TILES = 176
COUNT = MEMBERS * 2 * PAIRS
VMEM = 60 * 2**20


def dot(left, right, left_dim=1, right_dim=0):
    return lax.dot_general(
        left, right, (((left_dim,), (right_dim,)), ((), ())), preferred_element_type=F32
    )


def rows_of(ref, unit):
    return ref.at[unit // UNITS, :, pl.ds(unit % UNITS * COUNT, COUNT), :]


def pack_kernel(first, units, x_ref, cot_ref, out_ref, held, made, in_sems, out_sems):
    def arrival(n, which):
        source = rows_of((x_ref, cot_ref)[which], first + n)
        return pltpu.make_async_copy(source, held.at[n, which], in_sems.at[n, which])

    def departure(n):
        target = out_ref.at[:, :, pl.ds(n * PAIRS, PAIRS), :, :]
        return pltpu.make_async_copy(made.at[n], target, out_sems.at[n])

    for n in range(units):
        for which in range(2):
            arrival(n, which).start()
    for n in range(units):
        for which in range(2):
            arrival(n, which).wait()
            turned = jnp.swapaxes(held[n, which].astype(F32), 0, 1)
            made[n, :, which] = turned.reshape(MEMBERS, PAIRS, 16, C).astype(BF16)
        departure(n).start()
    for n in range(units):
        departure(n).wait()


def pack(alignment, cotangent, first, units):
    anywhere = pl.BlockSpec(memory_space=pl.ANY)
    return pl.pallas_call(
        functools.partial(pack_kernel, first, units),
        in_specs=[anywhere, anywhere],
        out_specs=anywhere,
        out_shape=pltpu.HBM((MEMBERS, 2, units * PAIRS, 16, C), BF16),
        scratch_shapes=[
            pltpu.VMEM((units, 2, OWN_ROWS, COUNT, C), BF16),
            pltpu.VMEM((units, MEMBERS, 2, PAIRS, 16, C), BF16),
            pltpu.SemaphoreType.DMA((units, 2)),
            pltpu.SemaphoreType.DMA((units,)),
        ],
        compiler_params=pltpu.CompilerParams(vmem_limit_bytes=VMEM),
        cost_estimate=pl.CostEstimate(flops=0, bytes_accessed=units * 2**20, transcendentals=0),
    )(alignment, cotangent)


def unpack_kernel(first, units, *refs):
    in_ref, upd_ref, grad_ref, held, made, in_sems, out_sems = refs[0], *refs[-6:]

    def arrival(n):
        source = in_ref.at[:, :, pl.ds(n * PAIRS, PAIRS), :, :]
        return pltpu.make_async_copy(source, held.at[n], in_sems.at[n])

    def departure(n, which):
        target = rows_of((upd_ref, grad_ref)[which], first + n)
        return pltpu.make_async_copy(made.at[n, which], target, out_sems.at[n, which])

    for n in range(units):
        arrival(n).start()
    for n in range(units):
        arrival(n).wait()
        for which in range(2):
            turned = held[n, :, which].astype(F32).reshape(COUNT, OWN_ROWS, C)
            made[n, which] = jnp.swapaxes(turned, 0, 1).astype(BF16)
            departure(n, which).start()
    for n in range(units):
        for which in range(2):
            departure(n, which).wait()


def unpack(packed, first, structs, earlier):
    anywhere = pl.BlockSpec(memory_space=pl.ANY)
    shape = pltpu.HBM((structs, OWN_ROWS, RES, C), BF16)
    units = packed.shape[2] // PAIRS
    return pl.pallas_call(
        functools.partial(unpack_kernel, first, units),
        in_specs=[anywhere] * (1 + len(earlier)),
        out_specs=[anywhere, anywhere],
        out_shape=[shape, shape],
        input_output_aliases={1 + k: k for k in range(len(earlier))},
        scratch_shapes=[
            pltpu.VMEM((units, MEMBERS, 2, PAIRS, 16, C), BF16),
            pltpu.VMEM((units, 2, OWN_ROWS, COUNT, C), BF16),
            pltpu.SemaphoreType.DMA((units,)),
            pltpu.SemaphoreType.DMA((units, 2)),
        ],
        compiler_params=pltpu.CompilerParams(vmem_limit_bytes=24 * 2**20),
        cost_estimate=pl.CostEstimate(flops=0, bytes_accessed=units * 2**20, transcendentals=0),
    )(packed, *earlier)


def token_rows(block):
    wide = block.astype(F32)
    return jnp.concatenate(
        [
            wide[:, pair, side : side + 8].reshape(ROWS, C)
            for pair in range(block.shape[1])
            for side in (0, 8)
        ],
        axis=0,
    )


def row_blocks(tokens, pair):
    first = tokens[2 * pair * ROWS : (2 * pair + 1) * ROWS].reshape(MEMBERS, 8, C)
    other = tokens[(2 * pair + 1) * ROWS : (2 * pair + 2) * ROWS].reshape(MEMBERS, 8, C)
    return jnp.concatenate([first, other], axis=1)


def fold_rows(tokens):
    return jnp.sum(tokens.reshape(tokens.shape[0] // 8, 8, C), axis=0)


def tiles_of(matrix):
    count = matrix.shape[0] // 8
    return matrix[:, :128].reshape(count, 8, 128), matrix[:, 128:].reshape(count, 8, 128)


def pair_kernel(steps, has_earlier, last, *refs):
    core_ref, x_ref, cot_ref, w_ref, wt_ref, wo_ref, gb_ref, rows_ref = refs[:8]
    qc, kc, vc, dac, attc, dprojc, gin, gout, vec, dlog = refs[-10:]
    if last:
        out_ref, own_ref, other_ref, sums_ref, refs = *refs[-14:-10], refs[:-10]
    else:
        out_ref, sums_ref = refs[-12:-10]

    @pl.when(pl.program_id(0) == 0)
    def _():
        gin[...] = jnp.zeros_like(gin)
        gout[...] = jnp.zeros_like(gout)
        vec[...] = jnp.zeros_like(vec)
        dlog[...] = jnp.zeros_like(dlog)

    pairs = x_ref.shape[2]
    out_bias, gain, bias = rows_ref[0:1], rows_ref[1:2], rows_ref[2:3]
    x = token_rows(x_ref[:, 0])
    cot = token_rows(cot_ref[:, 0])
    cot_half = cot.astype(BF16)
    centered = x - jnp.mean(x, axis=-1, keepdims=True)
    inv_std = lax.rsqrt(jnp.mean(centered * centered, axis=-1, keepdims=True) + EPSILON)
    standard = centered * inv_std
    normed = (standard * gain + bias).astype(BF16)

    kv = dot(normed, w_ref[:, HD : 3 * HD]).astype(BF16)
    proj = dot(wt_ref[...], normed, 1, 1)
    qc[...] = (proj[:HD] * INV_SCALE).astype(BF16)
    kc[...] = proj[HD : 2 * HD].astype(BF16)
    vc[...] = proj[2 * HD : 3 * HD].astype(BF16)
    gate = jax.nn.sigmoid(proj[3 * HD :] + jnp.concatenate([gb_ref[...]] * (2 * pairs), axis=1))
    d_gated = dot(wo_ref[...], cot_half, 1, 1)
    dac[...] = (d_gated * gate).astype(BF16)

    head_of_lane = lax.broadcasted_iota(jnp.int32, (1, 128), 1) // HDIM
    for r in range(2 * pairs):
        toks = slice(r * ROWS, (r + 1) * ROWS)
        for half in range(2):
            lanes = slice(half * 128, half * 128 + 128)
            k_half = kv[toks, half * 128 : half * 128 + 128]
            v_half = kv[toks, HD + half * 128 : HD + half * 128 + 128]
            zero = jnp.zeros_like(k_half)
            k_stack = jnp.concatenate(
                [jnp.where(head_of_lane == h, k_half, zero) for h in range(4)], axis=0
            )
            v_stack = jnp.concatenate(
                [jnp.where(head_of_lane == h, v_half, zero) for h in range(4)], axis=0
            )
            scores = dot(k_stack, qc[lanes, toks])
            d_softs = dot(v_stack, dac[lanes, toks])
            for hp in range(2):
                probs, d_ss = [], []
                for h in (2 * hp, 2 * hp + 1):
                    s = scores[h * 128 : h * 128 + 128]
                    d_soft = d_softs[h * 128 : h * 128 + 128]
                    shifted = jnp.exp(s - jnp.max(s, axis=0, keepdims=True))
                    soft = shifted * (1.0 / jnp.sum(shifted, axis=0, keepdims=True))
                    weighted = soft * d_soft
                    d_s = (weighted - soft * jnp.sum(weighted, axis=0, keepdims=True)).astype(BF16)
                    probs.append(soft.astype(BF16))
                    d_ss.append(d_s)
                probs = jnp.concatenate(probs, axis=0)
                d_ss = jnp.concatenate(d_ss, axis=0)
                f = half * 128 + hp * 2 * HDIM
                chans = slice(f, f + 2 * HDIM)
                hole = jnp.zeros((HDIM, ROWS), BF16)

                def diagonal(rows):
                    return jnp.concatenate(
                        [
                            jnp.concatenate([rows[:HDIM], hole], axis=1),
                            jnp.concatenate([hole, rows[HDIM:]], axis=1),
                        ],
                        axis=0,
                    )

                def blocks(wide):
                    return jnp.concatenate([wide[:HDIM, :ROWS], wide[HDIM:, ROWS:]], axis=0)

                attc[chans, toks] = dot(diagonal(vc[chans, toks]), probs)
                dprojc[chans, toks] = (dot(diagonal(kc[chans, toks]), d_ss) * INV_SCALE).astype(BF16)
                dprojc[HD + f : HD + f + 2 * HDIM, toks] = blocks(dot(qc[chans, toks], d_ss, 1, 1)).astype(BF16)
                dprojc[2 * HD + f : 2 * HD + f + 2 * HDIM, toks] = blocks(
                    dot(dac[chans, toks], probs, 1, 1)
                ).astype(BF16)


    gated = gate * attc[...]
    d_logit = (d_gated * gated * (1.0 - gate)).astype(BF16)
    dprojc[3 * HD :, :] = d_logit
    gated_half = gated.astype(BF16)
    wide_logit = d_logit.astype(F32)
    dlog[...] += functools.reduce(
        jnp.add, [wide_logit[:, r * ROWS : (r + 1) * ROWS] for r in range(2 * pairs)]
    )
    gin[...] += dot(dprojc[...], normed)
    gout[...] += dot(gated_half, cot_half)
    update = dot(gated_half.T, wo_ref[...]) + out_bias
    updated = x + update
    d_normed = dot(w_ref[...], dprojc[...]).T
    d_hat = d_normed * gain
    d_std = d_normed * standard
    branch = inv_std * (
        d_hat
        - jnp.mean(d_hat, axis=-1, keepdims=True)
        - standard * jnp.mean(d_hat * standard, axis=-1, keepdims=True)
    )
    grad = cot + branch
    for pair in range(pairs):
        out_ref[:, 0, pair] = row_blocks(updated, pair).astype(BF16)
        out_ref[:, 1, pair] = row_blocks(grad, pair).astype(BF16)
    vec[0] += fold_rows(cot)
    vec[1] += fold_rows(d_std)
    vec[2] += fold_rows(d_normed)

    @pl.when(pl.program_id(0) == steps - 1)
    def _():
        def put(half, first, tiles):
            count = tiles.shape[0]
            if has_earlier:
                tiles = tiles + refs[8][half, first : first + count]
            sums_ref[half, first : first + count] = tiles

        for block in range(5):
            matrix = gin[block * HD : (block + 1) * HD].T if block < 4 else gout[...]
            for half, tiles in enumerate(tiles_of(matrix)):
                put(half, block * 32, tiles)
        rows = [jnp.sum(dlog[...].T, axis=0, keepdims=True)] + [
            jnp.sum(vec[k], axis=0, keepdims=True) for k in range(3)
        ]
        vectors = [row[:, side : side + 128] for row in rows for side in (0, 128)]
        put(0, 160, jnp.concatenate(vectors, axis=0)[None])
        sums_ref[0, 161:] = jnp.zeros((TILES - 161, 8, 128), F32)
        sums_ref[1, 160:] = jnp.zeros((TILES - 160, 8, 128), F32)
        if last:
            core = core_ref[0]
            own_ref[...] = sums_ref[core]
            other_ref[...] = sums_ref[1 - core]


def columns(packed, core, params, steps, sums=None, last=False):
    pairs = packed.shape[2] // steps

    def part(which):
        return pl.BlockSpec((MEMBERS, 1, pairs, 16, C), lambda p: (0, which, p, 0, 0))

    def whole(shape):
        return pl.BlockSpec(shape, lambda p: (0,) * len(shape))

    half = (TILES, 8, 128)
    operands = [core, packed, packed, *params]
    in_specs = [pl.BlockSpec(memory_space=pltpu.SMEM), part(0), part(1)] + [whole(a.shape) for a in params]
    if sums is not None:
        operands.append(sums)
        in_specs.append(whole(sums.shape))
    out_specs = [pl.BlockSpec((MEMBERS, 2, pairs, 16, C), lambda p: (0, 0, p, 0, 0))]
    out_shape = [pltpu.HBM(packed.shape, BF16)]
    wide = (HD, 2 * pairs * ROWS)
    scratch = [pltpu.VMEM(wide, BF16)] * 4 + [
        pltpu.VMEM(wide, F32),
        pltpu.VMEM((4 * HD, 2 * pairs * ROWS), BF16),
        pltpu.VMEM((4 * HD, C), F32),
        pltpu.VMEM((HD, C), F32),
        pltpu.VMEM((3, 8, C), F32),
        pltpu.VMEM((HD, 128), F32),
    ]
    if last:
        out_specs += [whole(half)] * 2
        out_shape += [pltpu.HBM(half, F32)] * 2
        scratch.insert(0, pltpu.VMEM((2, *half), F32))
    else:
        out_specs.append(whole((2, *half)))
        out_shape.append(pltpu.HBM((2, *half), F32))
    return pl.pallas_call(
        functools.partial(pair_kernel, steps, sums is not None, last),
        grid=(steps,),
        in_specs=in_specs,
        out_specs=out_specs,
        out_shape=out_shape,
        scratch_shapes=scratch,
        compiler_params=pltpu.CompilerParams(
            dimension_semantics=("arbitrary",), vmem_limit_bytes=VMEM
        ),
        cost_estimate=pl.CostEstimate(
            flops=packed.shape[2] * 4_000_000_000, bytes_accessed=2**23, transcendentals=packed.shape[2] * 300_000
        ),
    )(*operands)


def shift(value, axes, size, step):
    return lax.ppermute(value, axes, [(k, (k + step) % size) for k in range(size)])


def scatter_sum(terms, axes, size):
    own = lax.axis_index(axes)
    count = terms[0].shape[0] // size

    def block_for(step):
        place = lax.rem(own + step, size) * count
        return functools.reduce(
            jnp.add, [lax.dynamic_slice_in_dim(term, place, count, 0) for term in terms]
        )

    arrived = [shift(block_for(step), axes, size, step) for step in range(1, size)]
    return functools.reduce(jnp.add, arrived, block_for(0))


def gather(value, axes, size):
    own = lax.axis_index(axes)
    count = value.shape[0]
    arrived = [shift(value, axes, size, step) for step in range(1, size)]
    total = jnp.zeros((size * count, *value.shape[1:]), value.dtype)
    for step, piece in enumerate([value, *arrived]):
        place = lax.rem(own + size - step, size) * count
        total = lax.dynamic_update_slice_in_dim(total, piece, place, 0)
    return total


def swap(value, axis):
    return lax.ppermute(value, axis, [(0, 1), (1, 0)])


def meet_sum(value, axes, size):
    own = lax.axis_index(axes)
    arrived = [shift(value, axes, size, step) for step in range(1, size)]
    met = jnp.concatenate([value, *arrived], axis=0).reshape(size, *value.shape)
    pieces = [
        lax.dynamic_index_in_dim(met, lax.rem(own + size - k, size), 0, keepdims=False)
        for k in range(size)
    ]
    return functools.reduce(jnp.add, pieces)


def finish_kernel(core_ref, own_ref, other_ref, mats_ref, out_ref, vec_ref):
    def write(halves):
        for half, ref in enumerate(halves):
            lanes = slice(half * 128, half * 128 + 128)
            for block in range(4):
                mats_ref[block, :, lanes] = ref[block * 32 : block * 32 + 32].reshape(C, 128)
            out_ref[:, lanes] = ref[128:160].reshape(C, 128)
        for k in range(8):
            vec_ref[k // 2 : k // 2 + 1, k % 2 * 128 : k % 2 * 128 + 128] = halves[0][160, k : k + 1]

    pl.when(core_ref[0] == 0)(lambda: write((own_ref, other_ref)))
    pl.when(core_ref[0] == 1)(lambda: write((other_ref, own_ref)))


def finish(core, own, other):
    vmem = pl.BlockSpec(memory_space=pltpu.VMEM)
    return pl.pallas_call(
        finish_kernel,
        in_specs=[pl.BlockSpec(memory_space=pltpu.SMEM), vmem, vmem],
        out_specs=[vmem] * 3,
        out_shape=[
            jax.ShapeDtypeStruct((4, C, HD), F32),
            jax.ShapeDtypeStruct((HD, C), F32),
            jax.ShapeDtypeStruct((4, C), F32),
        ],
        compiler_params=pltpu.CompilerParams(vmem_limit_bytes=16 * 2**20),
        cost_estimate=pl.CostEstimate(flops=0, bytes_accessed=2**22, transcendentals=0),
    )(core, own, other)


def rows_sum(own, other):
    tiles = scatter_sum([own, swap(other, "core")], "y", 4)
    return scatter_sum([tiles], "x", 4)


def shards(alignment, cotangent, wq, wk, wv, wg, gate_bias, wo, out_bias, gain, bias):
    structs = alignment.shape[0]
    w = jnp.concatenate([wq, wk, wv, wg], axis=1)
    rows = jnp.concatenate([jnp.stack([out_bias, gain, bias]), jnp.zeros((5, C), F32)], axis=0)
    params = (w, w.T, wo, jnp.broadcast_to(gate_bias[:, None], (HD, 128)), rows)
    core = lax.axis_index("core").reshape(1)
    after = lax.optimization_barrier

    def exchange(value):
        return lax.all_to_all(value, DAP, 0, 0, tiled=True)

    first = exchange(pack(alignment, cotangent, 0, 5))
    second = exchange(pack(alignment, cotangent, 5, 3))
    early, sums = columns(first, core, params, 2)
    early = exchange(early)
    late, own, other = columns(second, core, params, 1, sums, last=True)
    tiles = rows_sum(own, other)
    tiles = (tiles + swap(tiles, "z_hi")) * FACTOR
    tiles, late = after((meet_sum(tiles, "z_lo", 4), late))
    late = exchange(late)
    done = unpack(early, 0, structs, ())
    for axis in ("x", "y"):
        tiles = gather(tiles, axis, 4)
    mats, out, vectors = finish(core, tiles, swap(tiles, "core"))
    return (*unpack(late, 5, structs, tuple(done)), mats, out, vectors)


def solution(mesh):
    parts = Mesh(mesh.devices.reshape(2, 4, 2, 4, 4), BATCH + DAP)
    split = P(BATCH, DAP, None, None)
    return jax.shard_map(
        shards,
        mesh=parts,
        in_specs=(split, split) + (P(),) * 9,
        out_specs=(split, split, P(), P(), P()),
        check_vma=False,
    )
```
